512 devices in a mesh: space: 128 (over x_lo, y, z), chan: 4 (over x_hi, core).
Axes of the slice: x: 4 (x_hi: 2, x_lo: 2; x = x_hi * 2 + x_lo), y: 4, z: 16, core: 2. Of those that a mesh axis runs over, the one named last changes fastest.
Arguments:
- inputs: bfloat16 [2, 512, 256, 128], P(None, 'space', 'chan'), may hold values from -6 to 6
- weights: bfloat16 [3, 3, 256, 256], P(None, None, 'chan'), may hold values from -0.125 to 0.125
- target: bfloat16 [2, 512, 256, 128], P(None, 'space', 'chan'), may hold values from -15 to 15
Outputs:
- loss: float32 [], replicated
- grad_input: bfloat16 [2, 512, 256, 128], P(None, 'space', 'chan')
- weight_grad: float32 [3, 3, 256, 256], P(None, None, 'chan')
The draws below stay inside these ranges and needn't reach their ends.
All inputs are finite; a program needn't handle non-finite values.
Results may differ from the reference program's by a relative error of at most 0.0047.
Values may be sent and summed in bfloat16 or wider, within the bound.
No kernel may reach another device: no remote copies, remote signals or barrier semaphores. Data moves between devices by JAX's collectives and lax.ppermute only.
A program may use at most 64 MiB of HBM per device.

```python
import jax
import jax.numpy as jnp
from jax import lax

CHANNELS = 256
BATCH = 2
LAT = 128
LON = 512


def draw_target(key, part):
    key = jax.random.fold_in(key, 7)
    column = jnp.arange(LON, dtype=jnp.float32) / max(LON - 1, 1)
    base = jnp.clip(jax.random.normal(key, (BATCH, LON, CHANNELS, LAT), jnp.float32), -5.0, 5.0)
    values = base * (1.0 + 2.0 * column)[None, :, None, None]
    return values.astype(jnp.bfloat16)


def steps_of(rng, shape, split, low, high):
    level = 1.0
    for position, shards_of in split:
        steps = jax.random.uniform(jax.random.fold_in(jax.random.fold_in(rng, 6), position), (shards_of,), jnp.float32, low / len(split), high / len(split))
        level = level * jnp.repeat(jnp.exp(steps), shape[position] // shards_of).reshape((-1,) + (1,) * (len(shape) - 1 - position))
    return level


def normal_values(own_key, shape, width, limit, pieces=(), held_as=jnp.bfloat16):
    values = jax.random.normal(own_key, shape, jnp.float32) * width
    if len(pieces) > 0:
        values = steps_of(own_key, shape, pieces, -0.22, 0.18) * values
    return jnp.clip(values, min=-limit, max=limit).astype(held_as)


def setup_inputs(seed: int = 0) -> dict:
    key_of = jax.random.split(jax.random.key(seed), 4)
    inputs = normal_values(key_of[0], (BATCH, LON, CHANNELS, LAT), 1.0, 6.0, ((1, 128), (2, 4)))
    weights = normal_values(key_of[1], (3, 3, CHANNELS, CHANNELS), (9 * CHANNELS) ** -0.5, 0.125, ((2, 4),))
    target = draw_target(jax.random.fold_in(key_of[3], 71), 0)
    return {"inputs": inputs, "weights": weights, "target": target}


scale_factor = 64.0


def shifted(field, shift_lat, shift_lon):
    padded = jnp.pad(field, ((0, 0), (0, 0), (0, 0), (1, 1)))
    rows = padded[:, :, :, 1 + shift_lat:1 + shift_lat + LAT]
    return jnp.roll(rows, -shift_lon, axis=1)


def reference(inputs, weights, target):
    high = lax.Precision.HIGHEST
    predicted = jnp.zeros((BATCH, LON, CHANNELS, LAT), jnp.float32)
    for row_tap in range(3):
        for col_tap in range(3):
            moved = shifted(inputs, row_tap - 1, col_tap - 1).astype(jnp.float32)
            kernel = weights[row_tap, col_tap].astype(jnp.float32)
            predicted = predicted + jnp.einsum("bjci,cd->bjdi", moved, kernel, precision=high)
    coslat = jnp.cos(jnp.pi * ((jnp.arange(LAT, dtype=jnp.float32) + 0.5) / LAT - 0.5))
    weighting = coslat[None, None, None, :]
    diff = predicted - target.astype(jnp.float32)
    loss = 0.5 * jnp.sum(weighting * diff * diff) / (BATCH * LAT * LON * CHANNELS)
    cotangent = (weighting * diff).astype(jnp.bfloat16)
    cot_wide = cotangent.astype(jnp.float32)
    grad_sum = jnp.zeros((BATCH, LON, CHANNELS, LAT), jnp.float32)
    kernel_rows = []
    for row_tap in range(3):
        kernel_cols = []
        for col_tap in range(3):
            kernel = weights[row_tap, col_tap].astype(jnp.float32)
            back = shifted(cotangent, 1 - row_tap, 1 - col_tap).astype(jnp.float32)
            grad_sum = grad_sum + jnp.einsum("bjdi,cd->bjci", back, kernel, precision=high)
            moved = shifted(inputs, row_tap - 1, col_tap - 1).astype(jnp.float32)
            kernel_cols.append(jnp.einsum("bjci,bjdi->cd", moved, cot_wide, precision=high))
        kernel_rows.append(jnp.stack(kernel_cols))
    weight_grad = jnp.stack(kernel_rows) * (scale_factor / (BATCH * LAT * LON))
    grad_input = grad_sum.astype(jnp.bfloat16)
    return loss, grad_input, weight_grad
```

```python
import jax
import jax.numpy as jnp
from jax import lax
from jax.sharding import PartitionSpec as P

scale_factor = 64.0


def extended(block, sides, width):
    for axis, dim in sides:
        count = lax.axis_size(axis)
        forward = [(i, i + 1) for i in range(count - 1)]
        forward.append((count - 1, 0))
        backward = [(target, source) for source, target in forward]
        low = lax.ppermute(
            lax.slice_in_dim(block, block.shape[dim] - width, None, axis=dim), axis, forward
        )
        high = lax.ppermute(lax.slice_in_dim(block, 0, width, axis=dim), axis, backward)
        block = jnp.concatenate([low, block, high], axis=dim)
    return block


def tap_block(block, shift_lat, shift_lon, columns, rows):
    return block[
        :, 1 + shift_lon : 1 + shift_lon + columns, :, 1 + shift_lat : 1 + shift_lat + rows
    ]


def forward_terms(block, kernel, columns, rows):
    total = jnp.zeros((block.shape[0], columns, kernel.shape[3], rows), jnp.float32)
    for row_tap in range(3):
        for col_tap in range(3):
            moved = tap_block(block, row_tap - 1, col_tap - 1, columns, rows)
            total = total + jnp.einsum(
                "bjci,cd->bjdi", moved, kernel[row_tap, col_tap], preferred_element_type=jnp.float32
            )
    return total


def local(inputs, weights, target):
    batch_size, lon_cols, own_chan, lat_rows = inputs.shape
    channels = weights.shape[3]
    lon_total = lon_cols * lax.axis_size("space")
    rimmed = extended(inputs, (("space", 1),), 1)
    framed = jnp.pad(rimmed, ((0, 0), (0, 0), (0, 0), (1, 1)))
    partial = forward_terms(framed, weights, lon_cols, lat_rows)
    partial = partial.reshape(batch_size, lon_cols, channels // own_chan, own_chan, lat_rows)
    partial = jnp.moveaxis(partial, 2, 0)
    predicted = jnp.sum(lax.all_to_all(partial, "chan", 0, 0, tiled=True), axis=0)
    coslat = jnp.cos(jnp.pi * ((jnp.arange(lat_rows, dtype=jnp.float32) + 0.5) / lat_rows - 0.5))
    weighting = coslat[None, None, None, :]
    diff = predicted - target.astype(jnp.float32)
    partial_loss = 0.5 * jnp.sum(weighting * diff * diff)
    partial_loss = jnp.sum(lax.all_gather(jnp.full((8, 128), partial_loss), "chan")[:, 0, 0])
    cotangent = (weighting * diff).astype(jnp.bfloat16)
    cot_rim = extended(cotangent, (("space", 1),), 1)
    cot_framed = jnp.pad(cot_rim, ((0, 0), (0, 0), (0, 0), (1, 1)))
    start_grad = jnp.zeros((batch_size, lon_cols, own_chan, lat_rows), jnp.float32)
    piece = lax.all_gather(cot_framed, "chan", axis=2, tiled=True)
    grad_sum = start_grad
    centre = tap_block(piece, 0, 0, lon_cols, lat_rows)
    kernel_rows = []
    for row_tap in range(3):
        kernel_list = []
        for col_tap in range(3):
            back = tap_block(piece, 1 - row_tap, 1 - col_tap, lon_cols, lat_rows)
            grad_sum = grad_sum + jnp.einsum(
                "bjdi,cd->bjci", back, weights[row_tap, col_tap], preferred_element_type=jnp.float32
            )
            moved = tap_block(framed, row_tap - 1, col_tap - 1, lon_cols, lat_rows)
            kernel_list.append(
                jnp.einsum("bjci,bjdi->cd", moved, centre, preferred_element_type=jnp.float32)
            )
        kernel_rows.append(jnp.stack(kernel_list))
    fresh = jnp.stack(kernel_rows)
    count = lax.axis_size("space")
    parts = fresh.astype(jnp.bfloat16).reshape(count, 8, fresh.size // (8 * count))
    high = partial_loss.astype(jnp.bfloat16)
    low = (partial_loss - high.astype(jnp.float32)).astype(jnp.bfloat16)
    tail = jnp.broadcast_to(jnp.stack([high, low])[None, None, :], (count, 8, 2))
    parts = jnp.concatenate([parts, tail], axis=2)
    summed = jnp.sum(lax.all_to_all(parts, "space", 0, 0, tiled=True).astype(jnp.float32), axis=0)
    loss = (summed[0, -2] + summed[0, -1]) / (batch_size * lat_rows * lon_total * channels)
    own = (summed[:, :-2] * (scale_factor / (batch_size * lat_rows * lon_total))).astype(jnp.bfloat16)
    everyone = jnp.broadcast_to(own[None], (count,) + own.shape)
    weight_grad = lax.all_to_all(everyone, "space", 0, 0, tiled=True)
    weight_grad = weight_grad.astype(jnp.float32).reshape(fresh.shape)
    grad_input = grad_sum.astype(jnp.bfloat16)
    return (loss, grad_input, weight_grad)


def solution(mesh):
    in_specs = (
        P(None, "space", "chan", None),
        P(None, None, "chan", None),
        P(None, "space", "chan", None),
    )
    out_specs = (P(), P(None, "space", "chan", None), P(None, None, "chan", None))
    return jax.shard_map(local, mesh=mesh, in_specs=in_specs, out_specs=out_specs, check_vma=False)
```

```python
import jax
import jax.numpy as jnp
from jax import lax
from jax.experimental import pallas as pl
from jax.experimental.pallas import tpu as pltpu
from jax.sharding import Mesh
from jax.sharding import PartitionSpec as P

scale_factor = 64.0
SPACE = ("xlo", "y", "zhi", "zlo")
CHAN = ("xhi", "core")
NEAR = ("xlo", "y", "zlo")
BF16, F32 = jnp.bfloat16, jnp.float32


def shift_lanes(x, step):
    rows, lat = x.shape
    lane = lax.broadcasted_iota(jnp.int32, (rows, lat), 1)
    if step == 1:
        return jnp.where(lane == lat - 1, 0.0, pltpu.roll(x, lat - 1, 1))
    return jnp.where(lane == 0, 0.0, pltpu.roll(x, 1, 1))


def kernel(
    where_ref, own_ref, oth_ref, left_ref, right_ref, wt_ref, wown_ref, cos_ref,
    gi_ref, wg_ref, loss_ref, xs_ref, tg_ref, cot_ref,
):
    xhi, core = where_ref[0], where_ref[1]
    batch, cols, chans, lat = gi_ref.shape
    wide = batch * lat
    count = 2 * batch * cols
    rim = 3 * batch

    for chip in range(2):
        main = own_ref if chip == 0 else oth_ref
        for unit in range(2):
            block = chip * 2 + unit
            row = block * 3 * chans
            trow = pl.multiple_of(((chip ^ xhi) * 2 + unit) * chans, chans)
            base, edge = unit * count, (unit * 2 + chip) * rim
            for b in range(batch):
                for e in range(cols + 4):
                    if e < 2:
                        x = left_ref[edge + b * 2 + e]
                    elif e < cols + 2:
                        x = main[base + b * cols + e - 2]
                    else:
                        x = right_ref[edge + b * 2 + e - cols - 2]
                    at = pl.ds(e * wide + b * lat, lat)
                    x32 = x.astype(F32)
                    xs_ref[row : row + chans, at] = shift_lanes(x32, -1).astype(BF16)
                    xs_ref[row + chans : row + 2 * chans, at] = x
                    xs_ref[row + 2 * chans : row + 3 * chans, at] = shift_lanes(x32, 1).astype(BF16)
                for f in range(cols + 2):
                    if f < 1:
                        t = left_ref[edge + 2 * batch + b]
                    elif f < cols + 1:
                        t = main[base + (batch + b) * cols + f - 1]
                    else:
                        t = right_ref[edge + 2 * batch + b]
                    tg_ref[pl.ds(trow, chans), pl.ds(f * wide + b * lat, lat)] = t

    weighting = cos_ref[0:1, :]
    loss = jnp.zeros((8, wide), F32)
    for f in range(cols + 2):
        at = pl.ds(f * wide, wide)
        total = jnp.dot(wt_ref[0], xs_ref[:, at], preferred_element_type=F32)
        for q in (1, 2):
            total += jnp.dot(
                wt_ref[q], xs_ref[:, pl.ds((f + q) * wide, wide)], preferred_element_type=F32
            )
        diff = total - tg_ref[:, at].astype(F32)
        cot = weighting * diff
        cot_ref[:, at] = cot.astype(BF16)
        if 1 <= f <= cols:
            loss += jnp.sum((cot * diff).reshape(-1, 8, wide), axis=0)
    loss_ref[...] = jnp.full(loss_ref.shape, jnp.sum(loss), F32)

    for j in range(cols):
        total = jnp.zeros((3 * chans, wide), F32)
        for q in range(3):
            total += jnp.dot(
                wown_ref[q], cot_ref[:, pl.ds((j + 2 - q) * wide, wide)], preferred_element_type=F32
            )
        for b in range(batch):
            part = total[:, b * lat : (b + 1) * lat]
            grad = (
                shift_lanes(part[:chans], 1)
                + part[chans : 2 * chans]
                + shift_lanes(part[2 * chans :], -1)
            )
            gi_ref[b, j] = grad.astype(BF16)

    centre = cot_ref[:, wide : (cols + 1) * wide]
    mine = pl.ds(pl.multiple_of(core * 3 * chans, chans), 3 * chans)
    for q in range(3):
        wg_ref[q] = lax.dot_general(
            xs_ref[mine, pl.ds((q + 1) * wide, cols * wide)],
            centre,
            (((1,), (1,)), ((), ())),
            preferred_element_type=F32,
        )


def exchange(a, axes, count, to):
    return lax.ppermute(a, axes, [(i, to(i)) for i in range(count)])


def local(inputs, weights, target):
    batch, cols, chans, lat = inputs.shape
    channels = weights.shape[3]
    tiles = lax.axis_size(SPACE)
    lon = cols * tiles
    near, far = lax.axis_size(NEAR), lax.axis_size("zhi")
    xhi, core = lax.axis_index("xhi"), lax.axis_index("core")

    def gathered(a):
        return lax.all_gather(a, "core", axis=0, tiled=True)

    own = jnp.concatenate(
        [inputs.reshape(-1, chans, lat), target.reshape(-1, chans, lat)], axis=0
    )
    other = exchange(own, "xhi", 2, lambda i: 1 - i)
    w_other = exchange(weights, ("xlo", "xhi"), 4, lambda i: 3 - i)

    def edge(pack, side):
        both = pack.reshape(2, batch, cols, chans, lat)
        if side > 0:
            x, t = both[0, :, cols - 2 :], both[1, :, cols - 1 :]
        else:
            x, t = both[0, :, :2], both[1, :, :1]
        return [x.reshape(-1, chans, lat), t.reshape(-1, chans, lat)]

    to_right = jnp.concatenate(edge(own, 1) + edge(other, 1), axis=0)
    to_left = jnp.concatenate(edge(own, -1) + edge(other, -1), axis=0)
    left = exchange(to_right, SPACE, tiles, lambda i: (i + 1) % tiles)
    right = exchange(to_left, SPACE, tiles, lambda i: (i - 1) % tiles)

    w_mine, w_far = gathered(weights[None]), gathered(w_other[None])
    w_all = jnp.concatenate([w_mine, w_far], axis=0)
    wt = jnp.transpose(w_all, (2, 4, 0, 1, 3)).reshape(3, channels, 3 * channels)
    wown = jnp.transpose(weights, (1, 0, 2, 3)).reshape(3, 3 * chans, channels)

    coslat = jnp.cos(jnp.pi * ((jnp.arange(lat, dtype=F32) + 0.5) / lat - 0.5))
    cos_rows = jnp.broadcast_to(jnp.tile(coslat, batch)[None], (8, batch * lat))
    place = jnp.stack([xhi, core]).astype(jnp.int32)

    wide = batch * lat
    vmem = pl.BlockSpec(memory_space=pltpu.VMEM)
    grad_input, wg, loss_part = pl.pallas_call(
        kernel,
        out_shape=(
            jax.ShapeDtypeStruct((batch, cols, chans, lat), BF16),
            jax.ShapeDtypeStruct((3, 3 * chans, channels), F32),
            jax.ShapeDtypeStruct((8, 128), F32),
        ),
        in_specs=[pl.BlockSpec(memory_space=pltpu.SMEM)] + [vmem] * 7,
        out_specs=(vmem, vmem, vmem),
        scratch_shapes=[
            pltpu.VMEM((3 * channels, (cols + 4) * wide), BF16),
            pltpu.VMEM((channels, (cols + 2) * wide), BF16),
            pltpu.VMEM((channels, (cols + 2) * wide), BF16),
        ],
        compiler_params=pltpu.CompilerParams(vmem_limit_bytes=40 * 1024 * 1024),
        name="conv_all",
    )(place, gathered(own), gathered(other), gathered(left), gathered(right), wt, wown, cos_rows)

    half = channels // 2
    rows = 9 * chans * 2 // near
    parts = jnp.concatenate([wg[:, :, :half], wg[:, :, half:]], axis=0).reshape(near, rows, half)

    def with_loss(data, value):
        high = value.astype(BF16)
        low = (value - high.astype(F32)).astype(BF16)
        row = lax.broadcasted_iota(jnp.int32, (8, half), 0)
        block = jnp.where(row == 0, high, jnp.where(row == 1, low, jnp.zeros((), BF16)))
        block = jnp.broadcast_to(block, data.shape[:1] + block.shape)
        return jnp.concatenate([data.astype(BF16), block], axis=1)

    def everyone(a, axes):
        return lax.all_to_all(a, axes, 0, 0, tiled=True)

    first = everyone(with_loss(parts, loss_part[0, 0]), NEAR)
    total = jnp.sum(first.astype(F32), axis=0)
    value = total[rows, 0] + total[rows + 1, 0]
    second = everyone(
        with_loss(jnp.broadcast_to(total[None, :rows], (far, rows, half)), value), "zhi"
    )
    total = jnp.sum(second.astype(F32), axis=0)
    value = total[rows, 0] + total[rows + 1, 0]
    loss = 0.5 * value / (batch * lat * lon * channels)
    mine = (total[:rows] * (scale_factor / (batch * lat * lon))).astype(BF16)
    third = everyone(jnp.broadcast_to(mine[None], (near, rows, half)), NEAR)
    halves = third.reshape(2, 3, 3, chans, half).astype(F32)
    weight_grad = jnp.swapaxes(jnp.concatenate([halves[0], halves[1]], axis=-1), 0, 1)
    return (loss, grad_input, weight_grad)


def solution(mesh):
    grid = Mesh(mesh.devices.reshape(2, 4, 8, 2, 2, 2), SPACE + CHAN)
    in_specs = (
        P(None, SPACE, CHAN, None),
        P(None, None, CHAN, None),
        P(None, SPACE, CHAN, None),
    )
    out_specs = (P(), P(None, SPACE, CHAN, None), P(None, None, CHAN, None))
    return jax.shard_map(local, mesh=grid, in_specs=in_specs, out_specs=out_specs, check_vma=False)
```

```python
import jax
import jax.numpy as jnp
from jax import lax
from jax.experimental import pallas as pl
from jax.experimental.pallas import tpu as pltpu
from jax.sharding import Mesh
from jax.sharding import PartitionSpec as P

scale_factor = 64.0
SPACE = ("xlo", "y", "zhi", "zlo")
CHAN = ("xhi", "core")
NEAR = ("xlo", "y", "zlo")
BF16, F32 = jnp.bfloat16, jnp.float32


def shift_lanes(x, step):
    rows, lat = x.shape
    lane = lax.broadcasted_iota(jnp.int32, (rows, lat), 1)
    if step == 1:
        return jnp.where(lane == lat - 1, 0.0, pltpu.roll(x, lat - 1, 1))
    return jnp.where(lane == 0, 0.0, pltpu.roll(x, 1, 1))


def kernel(
    where_ref, own_ref, oth_ref, rim_ref, wt_ref, wown_ref, cos_ref,
    gi_ref, wg_ref, loss_ref, xs_ref, tg_ref, cot_ref,
):
    xhi, core = where_ref[0], where_ref[1]
    batch, cols, chans, lat = gi_ref.shape
    wide = batch * lat
    count = own_ref.shape[0] // 2
    rim = 3 * batch

    for chip in range(2):
        main = own_ref if chip == 0 else oth_ref
        for unit in range(2):
            block = chip * 2 + unit
            row = block * 3 * chans
            trow = pl.multiple_of(((chip ^ xhi) * 2 + unit) * chans, chans)
            base = unit * count
            left = (unit * 4 + chip) * rim
            right = left + 2 * rim
            for b in range(batch):
                for e in range(cols + 4):
                    if e < 2:
                        x = rim_ref[left + b * 2 + e]
                    elif e < cols + 2:
                        x = main[base + b * cols + e - 2]
                    else:
                        x = rim_ref[right + b * 2 + e - cols - 2]
                    at = pl.ds(e * wide + b * lat, lat)
                    x32 = x.astype(F32)
                    xs_ref[row : row + chans, at] = shift_lanes(x32, -1).astype(BF16)
                    xs_ref[row + chans : row + 2 * chans, at] = x
                    xs_ref[row + 2 * chans : row + 3 * chans, at] = shift_lanes(x32, 1).astype(BF16)
                for f in range(cols + 2):
                    if f < 1:
                        t = rim_ref[left + 2 * batch + b]
                    elif f < cols + 1:
                        t = main[base + (batch + b) * cols + f - 1]
                    else:
                        t = rim_ref[right + 2 * batch + b]
                    tg_ref[pl.ds(trow, chans), pl.ds(f * wide + b * lat, lat)] = t

    weighting = cos_ref[0:1, :]
    loss = jnp.zeros((8, wide), F32)
    for f in range(cols + 2):
        at = pl.ds(f * wide, wide)
        total = jnp.dot(wt_ref[0], xs_ref[:, at], preferred_element_type=F32)
        for q in (1, 2):
            total += jnp.dot(
                wt_ref[q], xs_ref[:, pl.ds((f + q) * wide, wide)], preferred_element_type=F32
            )
        diff = total - tg_ref[:, at].astype(F32)
        cot = weighting * diff
        cot_ref[:, at] = cot.astype(BF16)
        if 1 <= f <= cols:
            loss += jnp.sum((cot * diff).reshape(-1, 8, wide), axis=0)
    loss_ref[...] = jnp.full(loss_ref.shape, jnp.sum(loss), F32)

    for j in range(cols):
        total = jnp.zeros((3 * chans, wide), F32)
        for q in range(3):
            total += jnp.dot(
                wown_ref[q], cot_ref[:, pl.ds((j + 2 - q) * wide, wide)], preferred_element_type=F32
            )
        for b in range(batch):
            part = total[:, b * lat : (b + 1) * lat]
            grad = (
                shift_lanes(part[:chans], 1)
                + part[chans : 2 * chans]
                + shift_lanes(part[2 * chans :], -1)
            )
            gi_ref[b, j] = grad.astype(BF16)

    centre = cot_ref[:, wide : (cols + 1) * wide]
    mine = pl.ds(pl.multiple_of(core * 3 * chans, chans), 3 * chans)
    for q in range(3):
        fresh = lax.dot_general(
            xs_ref[mine, pl.ds((q + 1) * wide, cols * wide)],
            centre,
            (((1,), (1,)), ((), ())),
            preferred_element_type=F32,
        ).astype(BF16)
        half = wg_ref.shape[-1]
        for p in range(3):
            for h in range(2):
                wg_ref[h, p, q] = fresh[p * chans : (p + 1) * chans, h * half : (h + 1) * half]


def exchange(a, axes, count, to):
    return lax.ppermute(a, axes, [(i, to(i)) for i in range(count)])


def local(inputs, weights, target):
    batch, cols, chans, lat = inputs.shape
    channels = weights.shape[3]
    tiles = lax.axis_size(SPACE)
    lon = cols * tiles
    near, far = lax.axis_size(NEAR), lax.axis_size("zhi")
    xhi, core = lax.axis_index("xhi"), lax.axis_index("core")

    def gathered(a):
        return lax.all_gather(a, "core", axis=0, tiled=True)

    own = jnp.concatenate(
        [inputs.reshape(-1, chans, lat), target.reshape(-1, chans, lat)], axis=0
    )
    other = exchange(own, "xhi", 2, lambda i: 1 - i)
    w_other = exchange(weights, ("xlo", "xhi"), 4, lambda i: 3 - i)

    def edge(pack, side):
        both = pack.reshape(2, batch, cols, chans, lat)
        if side > 0:
            x, t = both[0, :, cols - 2 :], both[1, :, cols - 1 :]
        else:
            x, t = both[0, :, :2], both[1, :, :1]
        return [x.reshape(-1, chans, lat), t.reshape(-1, chans, lat)]

    to_right = jnp.concatenate(edge(own, 1) + edge(other, 1), axis=0)
    to_left = jnp.concatenate(edge(own, -1) + edge(other, -1), axis=0)
    left = exchange(to_right, SPACE, tiles, lambda i: (i + 1) % tiles)
    right = exchange(to_left, SPACE, tiles, lambda i: (i - 1) % tiles)

    half = channels // 2
    near_pack, far_pack = gathered(own), gathered(other)
    w_all = jnp.concatenate([gathered(weights[None]), gathered(w_other[None])], axis=0)
    wt = jnp.transpose(w_all, (2, 4, 0, 1, 3)).reshape(3, channels, 3 * channels)
    rim = gathered(jnp.concatenate([left, right], axis=0))
    wown = jnp.transpose(weights, (1, 0, 2, 3)).reshape(3, 3 * chans, channels)

    coslat = jnp.cos(jnp.pi * ((jnp.arange(lat, dtype=F32) + 0.5) / lat - 0.5))
    cos_rows = jnp.broadcast_to(jnp.tile(coslat, batch)[None], (8, batch * lat))
    place = jnp.stack([xhi, core]).astype(jnp.int32)

    wide = batch * lat
    vmem = pl.BlockSpec(memory_space=pltpu.VMEM)
    grad_input, wg, loss_part = pl.pallas_call(
        kernel,
        out_shape=(
            jax.ShapeDtypeStruct((batch, cols, chans, lat), BF16),
            jax.ShapeDtypeStruct((2, 3, 3, chans, half), BF16),
            jax.ShapeDtypeStruct((8, 128), F32),
        ),
        in_specs=[pl.BlockSpec(memory_space=pltpu.SMEM)] + [vmem] * 6,
        out_specs=(vmem, vmem, vmem),
        scratch_shapes=[
            pltpu.VMEM((3 * channels, (cols + 4) * wide), BF16),
            pltpu.VMEM((channels, (cols + 2) * wide), BF16),
            pltpu.VMEM((channels, (cols + 2) * wide), BF16),
        ],
        compiler_params=pltpu.CompilerParams(vmem_limit_bytes=16 * 1024 * 1024),
        name="conv_all",
    )(place, near_pack, far_pack, rim, wt, wown, cos_rows)

    rows = 9 * chans * 2 // near
    parts = wg.reshape(near, rows, half)

    def with_loss(data, value):
        high = value.astype(BF16)
        low = (value - high.astype(F32)).astype(BF16)
        row = lax.broadcasted_iota(jnp.int32, value.shape, 0)
        block = jnp.where(row < 4, high, low)
        block = jnp.broadcast_to(block, data.shape[:1] + block.shape)
        return jnp.concatenate([data.astype(BF16), block], axis=1)

    def everyone(a, axes):
        return lax.all_to_all(a, axes, 0, 0, tiled=True)

    def summed(a):
        total = jnp.sum(a.astype(F32), axis=0)
        value = total[rows : rows + 4] + total[rows + 4 :]
        return total[:rows], value

    total, value = summed(everyone(with_loss(parts, loss_part), NEAR))
    spread = jnp.broadcast_to(total[None], (far, rows, half))
    total, value = summed(
        everyone(with_loss(spread, jnp.concatenate([value, value], axis=0)), "zhi")
    )
    loss = 0.5 * value[0, 0] / (batch * lat * lon * channels)
    mine = (total * (scale_factor / (batch * lat * lon))).astype(BF16)
    third = everyone(jnp.broadcast_to(mine[None], (near, rows, half)), NEAR)
    halves = third.reshape(2, 3, 3, chans, half).astype(F32)
    weight_grad = jnp.concatenate([halves[0], halves[1]], axis=-1)
    return (loss, grad_input, weight_grad)


def solution(mesh):
    grid = Mesh(mesh.devices.reshape(2, 4, 8, 2, 2, 2), SPACE + CHAN)
    in_specs = (
        P(None, SPACE, CHAN, None),
        P(None, None, CHAN, None),
        P(None, SPACE, CHAN, None),
    )
    out_specs = (P(), P(None, SPACE, CHAN, None), P(None, None, CHAN, None))
    return jax.shard_map(local, mesh=grid, in_specs=in_specs, out_specs=out_specs, check_vma=False)
```

```python
import functools

import jax
import jax.numpy as jnp
from jax import lax
from jax.experimental import pallas as pl
from jax.experimental.pallas import tpu as pltpu
from jax.sharding import Mesh
from jax.sharding import PartitionSpec as P

scale_factor = 64.0
SPACE = ("xlo", "y", "zhi", "zlo")
CHAN = ("xhi", "core")
NEAR = ("xlo", "y", "zlo")
BF16, F32 = jnp.bfloat16, jnp.float32


def shift_lanes(x, step):
    rows, lat = x.shape
    lane = lax.broadcasted_iota(jnp.int32, (rows, lat), 1)
    if step == 1:
        return jnp.where(lane == lat - 1, 0.0, pltpu.roll(x, lat - 1, 1))
    return jnp.where(lane == 0, 0.0, pltpu.roll(x, 1, 1))


def place_block(xs_ref, row, at, x):
    chans = x.shape[0]
    wide = x.astype(F32)
    xs_ref[row : row + chans, at] = shift_lanes(wide, -1).astype(BF16)
    xs_ref[row + chans : row + 2 * chans, at] = x
    xs_ref[row + 2 * chans : row + 3 * chans, at] = shift_lanes(wide, 1).astype(BF16)


def early_kernel(early, near_ref, far_ref, w_ref, wt_ref, xs_ref, part_ref):
    chans, lat = near_ref.shape[1:]
    half = far_ref.shape[2]
    wide = part_ref.shape[1] // 6
    batch, cols = wide // lat, xs_ref.shape[1] // wide
    pack = (near_ref.shape[0] // 2, far_ref.shape[0] // 2)
    weights_at = batch * cols + early

    for q in range(3):
        blocks = []
        for block in range(4):
            unit = block % 2
            for p in range(3):
                if block < 2:
                    blocks.append(w_ref[unit * 3 + p, q])
                else:
                    first = unit * pack[1] + weights_at + p * 3 + q
                    blocks.append(jnp.concatenate([far_ref[first], far_ref[first + 9]], axis=1))
        for t in range(0, 12, 2):
            pair = jnp.concatenate(blocks[t : t + 2], axis=0)
            wt_ref[q, :, t * chans : (t + 2) * chans] = pair.T

    for block in range(4):
        unit, ref = block % 2, near_ref if block < 2 else far_ref
        for b in range(batch):
            for j in range(cols):
                x = ref[unit * pack[block // 2] + b * cols + j]
                place_block(xs_ref, block * 3 * chans, pl.ds(j * wide + b * lat, lat), x)

    for f in range(cols + 2):
        total = None
        for q in range(3):
            j = f + q - 2
            if 0 <= j < cols:
                term = jnp.dot(
                    wt_ref[q], xs_ref[:, j * wide : (j + 1) * wide], preferred_element_type=F32
                )
                total = term if total is None else total + term
        part_ref[:, f * wide : (f + 1) * wide] = total


def late_kernel(
    early, where_ref, near_ref, far_ref, rim_ref, wt_ref, xs_ref, part_ref, wown_ref, cos_ref,
    gi_ref, wg_ref, loss_ref, xh_ref, tg_ref, cot_ref,
):
    xhi, core = where_ref[0], where_ref[1]
    batch, cols, chans, lat = gi_ref.shape
    wide = batch * lat
    tile = batch * cols
    rim = 3 * batch
    pack = (near_ref.shape[0] // 2, far_ref.shape[0] // 2, rim_ref.shape[0] // 2)

    def outer(e):
        return e if e < 2 else e - cols

    for chip in range(2):
        for unit in range(2):
            row = (chip * 2 + unit) * 3 * chans
            trow = pl.multiple_of(((chip ^ xhi) * 2 + unit) * chans, chans)
            left = unit * pack[2] + chip * rim
            right = left + 2 * rim
            for b in range(batch):
                for e in (0, 1, cols + 2, cols + 3):
                    x = rim_ref[left + b * 2 + e] if e < 2 else rim_ref[right + b * 2 + e - cols - 2]
                    place_block(xh_ref, row, pl.ds(outer(e) * wide + b * lat, lat), x)
                for f in range(cols + 2):
                    own = b * cols + f - 1
                    if f < 1:
                        t = rim_ref[left + 2 * batch + b]
                    elif f > cols:
                        t = rim_ref[right + 2 * batch + b]
                    elif chip == 0:
                        t = near_ref[unit * pack[0] + tile + own]
                    elif own < early:
                        t = far_ref[unit * pack[1] + tile + own]
                    else:
                        t = rim_ref[unit * pack[2] + 4 * rim + own - early]
                    tg_ref[pl.ds(trow, chans), pl.ds(f * wide + b * lat, lat)] = t

    def column(e, rows):
        if 2 <= e < cols + 2:
            return xs_ref[rows, pl.ds((e - 2) * wide, wide)]
        return xh_ref[rows, pl.ds(outer(e) * wide, wide)]

    weighting = cos_ref[0:1, :]
    loss = jnp.zeros((8, wide), F32)
    for f in range(cols + 2):
        at = pl.ds(f * wide, wide)
        total = part_ref[:, at]
        for q in range(3):
            if not 2 <= f + q < cols + 2:
                total += jnp.dot(wt_ref[q], column(f + q, slice(None)), preferred_element_type=F32)
        diff = total - tg_ref[:, at].astype(F32)
        cot = weighting * diff
        cot_ref[:, at] = cot.astype(BF16)
        if 1 <= f <= cols:
            loss += jnp.sum((cot * diff).reshape(-1, 8, wide), axis=0)
    loss_ref[...] = jnp.full(loss_ref.shape, jnp.sum(loss), F32)

    for j in range(cols):
        total = jnp.zeros((3 * chans, wide), F32)
        for q in range(3):
            total += jnp.dot(
                wown_ref[q], cot_ref[:, pl.ds((j + 2 - q) * wide, wide)], preferred_element_type=F32
            )
        for b in range(batch):
            part = total[:, b * lat : (b + 1) * lat]
            grad = (
                shift_lanes(part[:chans], 1)
                + part[chans : 2 * chans]
                + shift_lanes(part[2 * chans :], -1)
            )
            gi_ref[b, j] = grad.astype(BF16)

    mine = pl.ds(pl.multiple_of(core * 3 * chans, chans), 3 * chans)
    half = wg_ref.shape[-1]
    for q in range(3):
        fresh = jnp.zeros((3 * chans, 2 * half), F32)
        for j in range(cols):
            fresh += lax.dot_general(
                column(q + j + 1, mine),
                cot_ref[:, pl.ds((j + 1) * wide, wide)],
                (((1,), (1,)), ((), ())),
                preferred_element_type=F32,
            )
        fresh = fresh.astype(BF16)
        for p in range(3):
            for h in range(2):
                wg_ref[h, p, q] = fresh[p * chans : (p + 1) * chans, h * half : (h + 1) * half]


def exchange(a, axes, count, to):
    return lax.ppermute(a, axes, [(i, to(i)) for i in range(count)])


def local(inputs, weights, target):
    batch, cols, chans, lat = inputs.shape
    channels = weights.shape[3]
    tiles = lax.axis_size(SPACE)
    lon = cols * tiles
    near, far = lax.axis_size(NEAR), lax.axis_size("zhi")
    xhi, core = lax.axis_index("xhi"), lax.axis_index("core")

    def gathered(a):
        return lax.all_gather(a, "core", axis=0, tiled=True)

    own = jnp.concatenate(
        [inputs.reshape(-1, chans, lat), target.reshape(-1, chans, lat)], axis=0
    )
    other = exchange(own, "xhi", 2, lambda i: 1 - i)
    w_other = exchange(weights, ("xlo", "xhi"), 4, lambda i: 3 - i)

    def edge(pack, side):
        both = pack.reshape(2, batch, cols, chans, lat)
        if side > 0:
            x, t = both[0, :, cols - 2 :], both[1, :, cols - 1 :]
        else:
            x, t = both[0, :, :2], both[1, :, :1]
        return [x.reshape(-1, chans, lat), t.reshape(-1, chans, lat)]

    to_right = jnp.concatenate(edge(own, 1) + edge(other, 1), axis=0)
    to_left = jnp.concatenate(edge(own, -1) + edge(other, -1), axis=0)
    left = exchange(to_right, SPACE, tiles, lambda i: (i + 1) % tiles)
    right = exchange(to_left, SPACE, tiles, lambda i: (i - 1) % tiles)

    half = channels // 2
    tile, early = batch * cols, 2
    near_pack = gathered(own)
    w_near = gathered(weights)
    w_far = w_other.reshape(9, chans, channels)
    far_pack = gathered(
        jnp.concatenate([other[: tile + early], w_far[:, :, :half], w_far[:, :, half:]], axis=0)
    )
    rim = gathered(jnp.concatenate([left, right, other[tile + early :]], axis=0))
    wown = jnp.transpose(weights, (1, 0, 2, 3)).reshape(3, 3 * chans, channels)

    coslat = jnp.cos(jnp.pi * ((jnp.arange(lat, dtype=F32) + 0.5) / lat - 0.5))
    cos_rows = jnp.broadcast_to(jnp.tile(coslat, batch)[None], (8, batch * lat))
    place = jnp.stack([xhi, core]).astype(jnp.int32)

    wide = batch * lat
    vmem = pl.BlockSpec(memory_space=pltpu.VMEM)
    wt, xs, part = pl.pallas_call(
        functools.partial(early_kernel, early),
        out_shape=(
            jax.ShapeDtypeStruct((3, channels, 3 * channels), BF16),
            jax.ShapeDtypeStruct((3 * channels, cols * wide), BF16),
            jax.ShapeDtypeStruct((channels, (cols + 2) * wide), F32),
        ),
        in_specs=[vmem] * 3,
        out_specs=(vmem, vmem, vmem),
        compiler_params=pltpu.CompilerParams(vmem_limit_bytes=16 * 1024 * 1024),
        cost_estimate=pl.CostEstimate(
            flops=24 * channels * channels * 3 * wide, bytes_accessed=6 << 20, transcendentals=0
        ),
        name="conv_tile",
    )(near_pack, far_pack, w_near)
    grad_input, wg, loss_part = pl.pallas_call(
        functools.partial(late_kernel, early),
        out_shape=(
            jax.ShapeDtypeStruct((batch, cols, chans, lat), BF16),
            jax.ShapeDtypeStruct((2, 3, 3, chans, half), BF16),
            jax.ShapeDtypeStruct((8, 128), F32),
        ),
        in_specs=[pl.BlockSpec(memory_space=pltpu.SMEM)] + [vmem] * 8,
        out_specs=(vmem, vmem, vmem),
        scratch_shapes=[
            pltpu.VMEM((3 * channels, 4 * wide), BF16),
            pltpu.VMEM((channels, (cols + 2) * wide), BF16),
            pltpu.VMEM((channels, (cols + 2) * wide), BF16),
        ],
        compiler_params=pltpu.CompilerParams(vmem_limit_bytes=16 * 1024 * 1024),
        name="conv_rim",
    )(place, near_pack, far_pack, rim, wt, xs, part, wown, cos_rows)

    rows = 9 * chans * 2 // near
    parts = wg.reshape(near, rows, half)

    def with_loss(data, value):
        high = value.astype(BF16)
        low = (value - high.astype(F32)).astype(BF16)
        row = lax.broadcasted_iota(jnp.int32, value.shape, 0)
        block = jnp.where(row < 4, high, low)
        block = jnp.broadcast_to(block, data.shape[:1] + block.shape)
        return jnp.concatenate([data.astype(BF16), block], axis=1)

    def everyone(a, axes):
        return lax.all_to_all(a, axes, 0, 0, tiled=True)

    def summed(a):
        total = jnp.sum(a.astype(F32), axis=0)
        value = total[rows : rows + 4] + total[rows + 4 :]
        return total[:rows], value

    total, value = summed(everyone(with_loss(parts, loss_part), NEAR))
    spread = jnp.broadcast_to(total[None], (far, rows, half))
    total, value = summed(
        everyone(with_loss(spread, jnp.concatenate([value, value], axis=0)), "zhi")
    )
    loss = 0.5 * value[0, 0] / (batch * lat * lon * channels)
    mine = (total * (scale_factor / (batch * lat * lon))).astype(BF16)
    third = everyone(jnp.broadcast_to(mine[None], (near, rows, half)), NEAR)
    halves = third.reshape(2, 3, 3, chans, half).astype(F32)
    weight_grad = jnp.concatenate([halves[0], halves[1]], axis=-1)
    return (loss, grad_input, weight_grad)


def solution(mesh):
    grid = Mesh(mesh.devices.reshape(2, 4, 8, 2, 2, 2), SPACE + CHAN)
    in_specs = (
        P(None, SPACE, CHAN, None),
        P(None, None, CHAN, None),
        P(None, SPACE, CHAN, None),
    )
    out_specs = (P(), P(None, SPACE, CHAN, None), P(None, None, CHAN, None))
    return jax.shard_map(local, mesh=grid, in_specs=in_specs, out_specs=out_specs, check_vma=False)
```

```python
import functools

import jax
import jax.numpy as jnp
from jax import lax
from jax.experimental import pallas as pl
from jax.experimental.pallas import tpu as pltpu
from jax.sharding import Mesh
from jax.sharding import PartitionSpec as P

scale_factor = 64.0
SPACE = ("xlo", "y", "zhi", "zlo")
CHAN = ("xhi", "core")
NEAR = ("xlo", "y", "zlo")
BF16, F32 = jnp.bfloat16, jnp.float32


def shift_lanes(x, step):
    rows, lat = x.shape
    lane = lax.broadcasted_iota(jnp.int32, (rows, lat), 1)
    if step == 1:
        return jnp.where(lane == lat - 1, 0.0, pltpu.roll(x, lat - 1, 1))
    return jnp.where(lane == 0, 0.0, pltpu.roll(x, 1, 1))


def place_block(xs_ref, row, at, x):
    chans = x.shape[0]
    wide = x.astype(F32)
    xs_ref[row : row + chans, at] = shift_lanes(wide, -1).astype(BF16)
    xs_ref[row + chans : row + 2 * chans, at] = x
    xs_ref[row + 2 * chans : row + 3 * chans, at] = shift_lanes(wide, 1).astype(BF16)


def pack_kernel(keep, pack_ref, w_ref, out_ref, rest_ref):
    half = out_ref.shape[2]
    out_ref[:keep] = pack_ref[:keep]
    rest_ref[...] = pack_ref[keep:]
    for p in range(3):
        for q in range(3):
            for h in range(2):
                out_ref[keep + h * 9 + p * 3 + q] = w_ref[p, q, :, h * half : (h + 1) * half]


def early_kernel(early, near_ref, far_ref, wt_ref, xs_ref, part_ref):
    chans, lat = near_ref.shape[1:]
    wide = part_ref.shape[1] // 6
    batch, cols = wide // lat, xs_ref.shape[1] // wide
    pack = near_ref.shape[0] // 2
    weights_at = batch * cols + early

    for q in range(3):
        blocks = []
        for block in range(4):
            unit, ref = block % 2, near_ref if block < 2 else far_ref
            for p in range(3):
                first = unit * pack + weights_at + p * 3 + q
                blocks.append(jnp.concatenate([ref[first], ref[first + 9]], axis=1))
        for t in range(0, 12, 2):
            pair = jnp.concatenate(blocks[t : t + 2], axis=0)
            wt_ref[q, :, t * chans : (t + 2) * chans] = pair.T

    for block in range(4):
        unit, ref = block % 2, near_ref if block < 2 else far_ref
        for b in range(batch):
            for j in range(cols):
                x = ref[unit * pack + b * cols + j]
                place_block(xs_ref, block * 3 * chans, pl.ds(j * wide + b * lat, lat), x)

    for f in range(cols + 2):
        total = None
        for q in range(3):
            j = f + q - 2
            if 0 <= j < cols:
                term = jnp.dot(
                    wt_ref[q], xs_ref[:, j * wide : (j + 1) * wide], preferred_element_type=F32
                )
                total = term if total is None else total + term
        part_ref[:, f * wide : (f + 1) * wide] = total


def late_kernel(
    early, where_ref, near_ref, far_ref, rim_ref, wt_ref, xs_ref, part_ref, wown_ref, cos_ref,
    gi_ref, wg_ref, loss_ref, xh_ref, tg_ref, cot_ref,
):
    xhi, core = where_ref[0], where_ref[1]
    batch, cols, chans, lat = gi_ref.shape
    wide = batch * lat
    tile = batch * cols
    rim = 3 * batch
    pack, rims = near_ref.shape[0] // 2, rim_ref.shape[0] // 2
    later = tile - early

    def outer(e):
        return e if e < 2 else e - cols

    for chip in range(2):
        for unit in range(2):
            row = (chip * 2 + unit) * 3 * chans
            trow = pl.multiple_of(((chip ^ xhi) * 2 + unit) * chans, chans)
            left = unit * rims + chip * rim
            main = near_ref if chip == 0 else far_ref
            right = left + 2 * rim
            for b in range(batch):
                for e in (0, 1, cols + 2, cols + 3):
                    x = rim_ref[left + b * 2 + e] if e < 2 else rim_ref[right + b * 2 + e - cols - 2]
                    place_block(xh_ref, row, pl.ds(outer(e) * wide + b * lat, lat), x)
                for f in range(cols + 2):
                    own = b * cols + f - 1
                    if f < 1:
                        t = rim_ref[left + 2 * batch + b]
                    elif f > cols:
                        t = rim_ref[right + 2 * batch + b]
                    elif own < early:
                        t = main[unit * pack + tile + own]
                    else:
                        t = rim_ref[unit * rims + 4 * rim + chip * later + own - early]
                    tg_ref[pl.ds(trow, chans), pl.ds(f * wide + b * lat, lat)] = t

    def column(e, rows):
        if 2 <= e < cols + 2:
            return xs_ref[rows, pl.ds((e - 2) * wide, wide)]
        return xh_ref[rows, pl.ds(outer(e) * wide, wide)]

    weighting = cos_ref[0:1, :]
    loss = jnp.zeros((8, wide), F32)
    for f in range(cols + 2):
        at = pl.ds(f * wide, wide)
        total = part_ref[:, at]
        for q in range(3):
            if not 2 <= f + q < cols + 2:
                total += jnp.dot(wt_ref[q], column(f + q, slice(None)), preferred_element_type=F32)
        diff = total - tg_ref[:, at].astype(F32)
        cot = weighting * diff
        cot_ref[:, at] = cot.astype(BF16)
        if 1 <= f <= cols:
            loss += jnp.sum((cot * diff).reshape(-1, 8, wide), axis=0)
    loss_ref[...] = jnp.full(loss_ref.shape, jnp.sum(loss), F32)

    for j in range(cols):
        total = jnp.zeros((3 * chans, wide), F32)
        for q in range(3):
            total += jnp.dot(
                wown_ref[q], cot_ref[:, pl.ds((j + 2 - q) * wide, wide)], preferred_element_type=F32
            )
        for b in range(batch):
            part = total[:, b * lat : (b + 1) * lat]
            grad = (
                shift_lanes(part[:chans], 1)
                + part[chans : 2 * chans]
                + shift_lanes(part[2 * chans :], -1)
            )
            gi_ref[b, j] = grad.astype(BF16)

    mine = pl.ds(pl.multiple_of(core * 3 * chans, chans), 3 * chans)
    half = wg_ref.shape[-1]
    for q in range(3):
        fresh = jnp.zeros((3 * chans, 2 * half), F32)
        for j in range(cols):
            fresh += lax.dot_general(
                column(q + j + 1, mine),
                cot_ref[:, pl.ds((j + 1) * wide, wide)],
                (((1,), (1,)), ((), ())),
                preferred_element_type=F32,
            )
        fresh = fresh.astype(BF16)
        for p in range(3):
            for h in range(2):
                wg_ref[h, p, q] = fresh[p * chans : (p + 1) * chans, h * half : (h + 1) * half]


def last_kernel(scale, halves_ref, value_ref, wg_ref, loss_ref):
    half = halves_ref.shape[-1]
    for h in range(2):
        wg_ref[:, :, :, h * half : (h + 1) * half] = halves_ref[h].astype(F32)
    loss_ref[0, 0] = jnp.max(value_ref[...]) * scale


def exchange(a, axes, count, to):
    return lax.ppermute(a, axes, [(i, to(i)) for i in range(count)])


def local(inputs, weights, target):
    batch, cols, chans, lat = inputs.shape
    channels = weights.shape[3]
    tiles = lax.axis_size(SPACE)
    lon = cols * tiles
    near, far = lax.axis_size(NEAR), lax.axis_size("zhi")
    xhi, core = lax.axis_index("xhi"), lax.axis_index("core")

    def gathered(a):
        return lax.all_gather(a, "core", axis=0, tiled=True)

    own = jnp.concatenate(
        [inputs.reshape(-1, chans, lat), target.reshape(-1, chans, lat)], axis=0
    )
    other = exchange(own, "xhi", 2, lambda i: 1 - i)
    w_other = exchange(weights, ("xlo", "xhi"), 4, lambda i: 3 - i)

    def edge(pack, side):
        both = pack.reshape(2, batch, cols, chans, lat)
        if side > 0:
            x, t = both[0, :, cols - 2 :], both[1, :, cols - 1 :]
        else:
            x, t = both[0, :, :2], both[1, :, :1]
        return [x.reshape(-1, chans, lat), t.reshape(-1, chans, lat)]

    to_right = jnp.concatenate(edge(own, 1) + edge(other, 1), axis=0)
    to_left = jnp.concatenate(edge(own, -1) + edge(other, -1), axis=0)
    left = exchange(to_right, SPACE, tiles, lambda i: (i + 1) % tiles)
    right = exchange(to_left, SPACE, tiles, lambda i: (i - 1) % tiles)

    half = channels // 2
    tile, early = batch * cols, 5

    keep = tile + early
    vmem = pl.BlockSpec(memory_space=pltpu.VMEM)

    def with_weights(pack, w):
        return pl.pallas_call(
            functools.partial(pack_kernel, keep),
            out_shape=(
                jax.ShapeDtypeStruct((keep + 18, chans, half), BF16),
                jax.ShapeDtypeStruct((2 * tile - keep, chans, half), BF16),
            ),
            in_specs=[vmem] * 2,
            out_specs=(vmem, vmem),
            compiler_params=pltpu.CompilerParams(vmem_limit_bytes=8 * 1024 * 1024),
            cost_estimate=pl.CostEstimate(flops=0, bytes_accessed=1 << 20, transcendentals=0),
            name="pack",
        )(pack, w)

    near_part, near_rest = with_weights(own, weights)
    far_part, far_rest = with_weights(other, w_other)
    near_pack, far_pack = gathered(near_part), gathered(far_part)
    rim = gathered(jnp.concatenate([left, right, near_rest, far_rest], axis=0))
    wown = jnp.transpose(weights, (1, 0, 2, 3)).reshape(3, 3 * chans, channels)

    coslat = jnp.cos(jnp.pi * ((jnp.arange(lat, dtype=F32) + 0.5) / lat - 0.5))
    cos_rows = jnp.broadcast_to(jnp.tile(coslat, batch)[None], (8, batch * lat))
    place = jnp.stack([xhi, core]).astype(jnp.int32)

    wide = batch * lat
    wt, xs, part = pl.pallas_call(
        functools.partial(early_kernel, early),
        out_shape=(
            jax.ShapeDtypeStruct((3, channels, 3 * channels), BF16),
            jax.ShapeDtypeStruct((3 * channels, cols * wide), BF16),
            jax.ShapeDtypeStruct((channels, (cols + 2) * wide), F32),
        ),
        in_specs=[vmem] * 2,
        out_specs=(vmem, vmem, vmem),
        compiler_params=pltpu.CompilerParams(vmem_limit_bytes=16 * 1024 * 1024),
        cost_estimate=pl.CostEstimate(
            flops=24 * channels * channels * 3 * wide, bytes_accessed=6 << 20, transcendentals=0
        ),
        name="conv_tile",
    )(near_pack, far_pack)
    grad_input, wg, loss_part = pl.pallas_call(
        functools.partial(late_kernel, early),
        out_shape=(
            jax.ShapeDtypeStruct((batch, cols, chans, lat), BF16),
            jax.ShapeDtypeStruct((2, 3, 3, chans, half), BF16),
            jax.ShapeDtypeStruct((8, 128), F32),
        ),
        in_specs=[pl.BlockSpec(memory_space=pltpu.SMEM)] + [vmem] * 8,
        out_specs=(vmem, vmem, vmem),
        scratch_shapes=[
            pltpu.VMEM((3 * channels, 4 * wide), BF16),
            pltpu.VMEM((channels, (cols + 2) * wide), BF16),
            pltpu.VMEM((channels, (cols + 2) * wide), BF16),
        ],
        compiler_params=pltpu.CompilerParams(vmem_limit_bytes=16 * 1024 * 1024),
        name="conv_rim",
    )(place, near_pack, far_pack, rim, wt, xs, part, wown, cos_rows)

    rows = 9 * chans * 2 // near
    parts = wg.reshape(near, rows, half)

    def with_loss(data, value):
        high = value.astype(BF16)
        low = (value - high.astype(F32)).astype(BF16)
        row = lax.broadcasted_iota(jnp.int32, value.shape, 0)
        block = jnp.where(row < 4, high, low)
        block = jnp.broadcast_to(block, data.shape[:1] + block.shape)
        return jnp.concatenate([data.astype(BF16), block], axis=1)

    def everyone(a, axes):
        return lax.all_to_all(a, axes, 0, 0, tiled=True)

    def summed(a):
        total = jnp.sum(a.astype(F32), axis=0)
        value = total[rows : rows + 4] + total[rows + 4 :]
        return total[:rows], value

    total, value = summed(everyone(with_loss(parts, loss_part), NEAR))
    spread = jnp.broadcast_to(total[None], (far, rows, half))
    total, value = summed(
        everyone(with_loss(spread, jnp.concatenate([value, value], axis=0)), "zhi")
    )
    mine = (total * (scale_factor / (batch * lat * lon))).astype(BF16)
    third = everyone(jnp.broadcast_to(mine[None], (near, rows, half)), NEAR)
    weight_grad, loss = pl.pallas_call(
        functools.partial(last_kernel, 0.5 / (batch * lat * lon * channels)),
        out_shape=(
            jax.ShapeDtypeStruct(weights.shape, F32),
            jax.ShapeDtypeStruct((1, 1), F32),
        ),
        in_specs=[vmem] * 2,
        out_specs=(vmem, pl.BlockSpec(memory_space=pltpu.SMEM)),
        compiler_params=pltpu.CompilerParams(vmem_limit_bytes=8 * 1024 * 1024),
        name="widen",
    )(third.reshape(2, 3, 3, chans, half), value)
    return (loss[0, 0], grad_input, weight_grad)


def solution(mesh):
    grid = Mesh(mesh.devices.reshape(2, 4, 8, 2, 2, 2), SPACE + CHAN)
    in_specs = (
        P(None, SPACE, CHAN, None),
        P(None, None, CHAN, None),
        P(None, SPACE, CHAN, None),
    )
    out_specs = (P(), P(None, SPACE, CHAN, None), P(None, None, CHAN, None))
    return jax.shard_map(local, mesh=grid, in_specs=in_specs, out_specs=out_specs, check_vma=False)
```

```python
import functools

import jax
import jax.numpy as jnp
from jax import lax
from jax.experimental import pallas as pl
from jax.experimental.pallas import tpu as pltpu
from jax.sharding import Mesh
from jax.sharding import PartitionSpec as P

scale_factor = 64.0
SPACE = ("xlo", "y", "zhi", "zlo")
CHAN = ("xhi", "core")
NEAR = ("xlo", "y", "zlo")
BF16, F32 = jnp.bfloat16, jnp.float32


def shift_lanes(x, step):
    rows, lat = x.shape
    lane = lax.broadcasted_iota(jnp.int32, (rows, lat), 1)
    if step == 1:
        return jnp.where(lane == lat - 1, 0.0, pltpu.roll(x, lat - 1, 1))
    return jnp.where(lane == 0, 0.0, pltpu.roll(x, 1, 1))


def place_block(xs_ref, row, at, x):
    chans = x.shape[0]
    wide = x.astype(F32)
    xs_ref[row : row + chans, at] = shift_lanes(wide, -1).astype(BF16)
    xs_ref[row + chans : row + 2 * chans, at] = x
    xs_ref[row + 2 * chans : row + 3 * chans, at] = shift_lanes(wide, 1).astype(BF16)


def pack_kernel(keep, pack_ref, w_ref, out_ref, rest_ref):
    half = out_ref.shape[2]
    out_ref[:keep] = pack_ref[:keep]
    rest_ref[...] = pack_ref[keep:]
    for p in range(3):
        for q in range(3):
            for h in range(2):
                out_ref[keep + h * 9 + p * 3 + q] = w_ref[p, q, :, h * half : (h + 1) * half]


def early_kernel(early, near_ref, far_ref, wt_ref, xs_ref, part_ref):
    chans, lat = near_ref.shape[1:]
    wide = part_ref.shape[1] // 6
    batch, cols = wide // lat, xs_ref.shape[1] // wide
    pack = near_ref.shape[0] // 2
    weights_at = batch * cols + early

    for q in range(3):
        blocks = []
        for block in range(4):
            unit, ref = block % 2, near_ref if block < 2 else far_ref
            for p in range(3):
                first = unit * pack + weights_at + p * 3 + q
                blocks.append(jnp.concatenate([ref[first], ref[first + 9]], axis=1))
        for t in range(0, 12, 2):
            pair = jnp.concatenate(blocks[t : t + 2], axis=0)
            wt_ref[q, :, t * chans : (t + 2) * chans] = pair.T

    for block in range(4):
        unit, ref = block % 2, near_ref if block < 2 else far_ref
        for b in range(batch):
            for j in range(cols):
                x = ref[unit * pack + b * cols + j]
                place_block(xs_ref, block * 3 * chans, pl.ds(j * wide + b * lat, lat), x)

    for f in range(cols + 2):
        total = None
        for q in range(3):
            j = f + q - 2
            if 0 <= j < cols:
                term = jnp.dot(
                    wt_ref[q], xs_ref[:, j * wide : (j + 1) * wide], preferred_element_type=F32
                )
                total = term if total is None else total + term
        part_ref[:, f * wide : (f + 1) * wide] = total


def late_kernel(
    early, where_ref, near_ref, far_ref, rim_ref, wt_ref, xs_ref, part_ref, wown_ref, cos_ref,
    gi_ref, wg_ref, loss_ref, xh_ref, tg_ref, cot_ref, grad_ref, sem,
):
    xhi, core = where_ref[0], where_ref[1]
    batch, cols, chans, lat = gi_ref.shape
    wide = batch * lat
    tile = batch * cols
    rim = 3 * batch
    pack, rims = near_ref.shape[0] // 2, rim_ref.shape[0] // 2
    later = tile - early

    def outer(e):
        return e if e < 2 else e - cols

    for chip in range(2):
        for unit in range(2):
            row = (chip * 2 + unit) * 3 * chans
            trow = pl.multiple_of(((chip ^ xhi) * 2 + unit) * chans, chans)
            left = unit * rims + chip * rim
            main = near_ref if chip == 0 else far_ref
            right = left + 2 * rim
            for b in range(batch):
                for e in (0, 1, cols + 2, cols + 3):
                    x = rim_ref[left + b * 2 + e] if e < 2 else rim_ref[right + b * 2 + e - cols - 2]
                    place_block(xh_ref, row, pl.ds(outer(e) * wide + b * lat, lat), x)
                for f in range(cols + 2):
                    own = b * cols + f - 1
                    if f < 1:
                        t = rim_ref[left + 2 * batch + b]
                    elif f > cols:
                        t = rim_ref[right + 2 * batch + b]
                    elif own < early:
                        t = main[unit * pack + tile + own]
                    else:
                        t = rim_ref[unit * rims + 4 * rim + chip * later + own - early]
                    tg_ref[pl.ds(trow, chans), pl.ds(f * wide + b * lat, lat)] = t

    def column(e, rows):
        if 2 <= e < cols + 2:
            return xs_ref[rows, pl.ds((e - 2) * wide, wide)]
        return xh_ref[rows, pl.ds(outer(e) * wide, wide)]

    weighting = cos_ref[0:1, :]
    loss = jnp.zeros((8, wide), F32)
    for f in range(cols + 2):
        at = pl.ds(f * wide, wide)
        total = part_ref[:, at]
        for q in range(3):
            if not 2 <= f + q < cols + 2:
                total += jnp.dot(wt_ref[q], column(f + q, slice(None)), preferred_element_type=F32)
        diff = total - tg_ref[:, at].astype(F32)
        cot = weighting * diff
        cot_ref[:, at] = cot.astype(BF16)
        if 1 <= f <= cols:
            loss += jnp.sum((cot * diff).reshape(-1, 8, wide), axis=0)
    loss_ref[...] = jnp.full(loss_ref.shape, jnp.sum(loss), F32)

    for j in range(cols):
        total = jnp.zeros((3 * chans, wide), F32)
        for q in range(3):
            total += jnp.dot(
                wown_ref[q], cot_ref[:, pl.ds((j + 2 - q) * wide, wide)], preferred_element_type=F32
            )
        for b in range(batch):
            part = total[:, b * lat : (b + 1) * lat]
            grad = (
                shift_lanes(part[:chans], 1)
                + part[chans : 2 * chans]
                + shift_lanes(part[2 * chans :], -1)
            )
            grad_ref[b, j] = grad.astype(BF16)
    leaving = pltpu.make_async_copy(grad_ref, gi_ref, sem)
    leaving.start()

    mine = pl.ds(pl.multiple_of(core * 3 * chans, chans), 3 * chans)
    half = wg_ref.shape[-1]
    for q in range(3):
        fresh = jnp.zeros((3 * chans, 2 * half), F32)
        for j in range(cols):
            fresh += lax.dot_general(
                column(q + j + 1, mine),
                cot_ref[:, pl.ds((j + 1) * wide, wide)],
                (((1,), (1,)), ((), ())),
                preferred_element_type=F32,
            )
        fresh = fresh.astype(BF16)
        for p in range(3):
            for h in range(2):
                wg_ref[h, p, q] = fresh[p * chans : (p + 1) * chans, h * half : (h + 1) * half]
    leaving.wait()


def last_kernel(scale, halves_ref, value_ref, wg_ref, loss_ref):
    half = halves_ref.shape[-1]
    for h in range(2):
        wg_ref[:, :, :, h * half : (h + 1) * half] = halves_ref[h].astype(F32)
    loss_ref[0, 0] = jnp.max(value_ref[...]) * scale


def exchange(a, axes, count, to):
    return lax.ppermute(a, axes, [(i, to(i)) for i in range(count)])


def local(inputs, weights, target):
    batch, cols, chans, lat = inputs.shape
    channels = weights.shape[3]
    tiles = lax.axis_size(SPACE)
    lon = cols * tiles
    near, far = lax.axis_size(NEAR), lax.axis_size("zhi")
    xhi, core = lax.axis_index("xhi"), lax.axis_index("core")

    def gathered(a):
        return lax.all_gather(a, "core", axis=0, tiled=True)

    own = jnp.concatenate(
        [inputs.reshape(-1, chans, lat), target.reshape(-1, chans, lat)], axis=0
    )
    other = exchange(own, "xhi", 2, lambda i: 1 - i)
    w_other = exchange(weights, ("xlo", "xhi"), 4, lambda i: 3 - i)

    def edge(pack, side):
        both = pack.reshape(2, batch, cols, chans, lat)
        if side > 0:
            x, t = both[0, :, cols - 2 :], both[1, :, cols - 1 :]
        else:
            x, t = both[0, :, :2], both[1, :, :1]
        return [x.reshape(-1, chans, lat), t.reshape(-1, chans, lat)]

    to_right = jnp.concatenate(edge(own, 1) + edge(other, 1), axis=0)
    to_left = jnp.concatenate(edge(own, -1) + edge(other, -1), axis=0)
    left = exchange(to_right, SPACE, tiles, lambda i: (i + 1) % tiles)
    right = exchange(to_left, SPACE, tiles, lambda i: (i - 1) % tiles)

    half = channels // 2
    tile, early = batch * cols, 5

    keep = tile + early
    vmem = pl.BlockSpec(memory_space=pltpu.VMEM)

    def with_weights(pack, w):
        return pl.pallas_call(
            functools.partial(pack_kernel, keep),
            out_shape=(
                jax.ShapeDtypeStruct((keep + 18, chans, half), BF16),
                jax.ShapeDtypeStruct((2 * tile - keep, chans, half), BF16),
            ),
            in_specs=[vmem] * 2,
            out_specs=(vmem, vmem),
            compiler_params=pltpu.CompilerParams(vmem_limit_bytes=8 * 1024 * 1024),
            cost_estimate=pl.CostEstimate(flops=0, bytes_accessed=1 << 20, transcendentals=0),
            name="pack",
        )(pack, w)

    near_part, near_rest = with_weights(own, weights)
    far_part, far_rest = with_weights(other, w_other)
    near_pack, far_pack = gathered(near_part), gathered(far_part)
    rim = gathered(jnp.concatenate([left, right, near_rest, far_rest], axis=0))
    wown = jnp.transpose(weights, (1, 0, 2, 3)).reshape(3, 3 * chans, channels)

    coslat = jnp.cos(jnp.pi * ((jnp.arange(lat, dtype=F32) + 0.5) / lat - 0.5))
    cos_rows = jnp.broadcast_to(jnp.tile(coslat, batch)[None], (8, batch * lat))
    place = jnp.stack([xhi, core]).astype(jnp.int32)

    wide = batch * lat
    wt, xs, part = pl.pallas_call(
        functools.partial(early_kernel, early),
        out_shape=(
            jax.ShapeDtypeStruct((3, channels, 3 * channels), BF16),
            jax.ShapeDtypeStruct((3 * channels, cols * wide), BF16),
            jax.ShapeDtypeStruct((channels, (cols + 2) * wide), F32),
        ),
        in_specs=[vmem] * 2,
        out_specs=(vmem, vmem, vmem),
        compiler_params=pltpu.CompilerParams(vmem_limit_bytes=16 * 1024 * 1024),
        cost_estimate=pl.CostEstimate(
            flops=24 * channels * channels * 3 * wide, bytes_accessed=6 << 20, transcendentals=0
        ),
        name="conv_tile",
    )(near_pack, far_pack)
    grad_input, wg, loss_part = pl.pallas_call(
        functools.partial(late_kernel, early),
        out_shape=(
            jax.ShapeDtypeStruct((batch, cols, chans, lat), BF16),
            jax.ShapeDtypeStruct((2, 3, 3, chans, half), BF16),
            jax.ShapeDtypeStruct((8, 128), F32),
        ),
        in_specs=[pl.BlockSpec(memory_space=pltpu.SMEM)] + [vmem] * 8,
        out_specs=(pl.BlockSpec(memory_space=pl.ANY), vmem, vmem),
        scratch_shapes=[
            pltpu.VMEM((3 * channels, 4 * wide), BF16),
            pltpu.VMEM((channels, (cols + 2) * wide), BF16),
            pltpu.VMEM((channels, (cols + 2) * wide), BF16),
            pltpu.VMEM((batch, cols, chans, lat), BF16),
            pltpu.SemaphoreType.DMA,
        ],
        compiler_params=pltpu.CompilerParams(vmem_limit_bytes=16 * 1024 * 1024),
        name="conv_rim",
    )(place, near_pack, far_pack, rim, wt, xs, part, wown, cos_rows)

    rows = 9 * chans * 2 // near
    parts = wg.reshape(near, rows, half)

    def with_loss(data, value):
        high = value.astype(BF16)
        low = (value - high.astype(F32)).astype(BF16)
        row = lax.broadcasted_iota(jnp.int32, value.shape, 0)
        block = jnp.where(row < 4, high, low)
        block = jnp.broadcast_to(block, data.shape[:1] + block.shape)
        return jnp.concatenate([data.astype(BF16), block], axis=1)

    def everyone(a, axes):
        return lax.all_to_all(a, axes, 0, 0, tiled=True)

    def summed(a):
        total = jnp.sum(a.astype(F32), axis=0)
        value = total[rows : rows + 4] + total[rows + 4 :]
        return total[:rows], value

    total, value = summed(everyone(with_loss(parts, loss_part), NEAR))
    spread = jnp.broadcast_to(total[None], (far, rows, half))
    total, value = summed(
        everyone(with_loss(spread, jnp.concatenate([value, value], axis=0)), "zhi")
    )
    total, value = lax.optimization_barrier((total, value))
    mine = (total * (scale_factor / (batch * lat * lon))).astype(BF16)
    third = everyone(jnp.broadcast_to(mine[None], (near, rows, half)), NEAR)
    weight_grad, loss = pl.pallas_call(
        functools.partial(last_kernel, 0.5 / (batch * lat * lon * channels)),
        out_shape=(
            jax.ShapeDtypeStruct(weights.shape, F32),
            jax.ShapeDtypeStruct((1, 1), F32),
        ),
        in_specs=[vmem] * 2,
        out_specs=(vmem, pl.BlockSpec(memory_space=pltpu.SMEM)),
        compiler_params=pltpu.CompilerParams(vmem_limit_bytes=8 * 1024 * 1024),
        name="widen",
    )(third.reshape(2, 3, 3, chans, half), value)
    return (loss[0, 0], grad_input, weight_grad)


def solution(mesh):
    grid = Mesh(mesh.devices.reshape(2, 4, 8, 2, 2, 2), SPACE + CHAN)
    in_specs = (
        P(None, SPACE, CHAN, None),
        P(None, None, CHAN, None),
        P(None, SPACE, CHAN, None),
    )
    out_specs = (P(), P(None, SPACE, CHAN, None), P(None, None, CHAN, None))
    return jax.shard_map(local, mesh=grid, in_specs=in_specs, out_specs=out_specs, check_vma=False)
```

```python
import functools

import jax
import jax.numpy as jnp
from jax import lax
from jax.experimental import pallas as pl
from jax.experimental.pallas import tpu as pltpu
from jax.sharding import Mesh
from jax.sharding import PartitionSpec as P

scale_factor = 64.0
SPACE = ("xlo", "y", "zhi", "zlo")
CHAN = ("xhi", "core")
NEAR = ("xlo", "y", "zlo")
BF16, F32 = jnp.bfloat16, jnp.float32


def shift_lanes(x, step):
    rows, lat = x.shape
    lane = lax.broadcasted_iota(jnp.int32, (rows, lat), 1)
    if step == 1:
        return jnp.where(lane == lat - 1, 0.0, pltpu.roll(x, lat - 1, 1))
    return jnp.where(lane == 0, 0.0, pltpu.roll(x, 1, 1))


def place_block(xs_ref, row, at, x):
    chans = x.shape[0]
    wide = x.astype(F32)
    xs_ref[row : row + chans, at] = shift_lanes(wide, -1).astype(BF16)
    xs_ref[row + chans : row + 2 * chans, at] = x
    xs_ref[row + 2 * chans : row + 3 * chans, at] = shift_lanes(wide, 1).astype(BF16)


def pack_kernel(keep, pack_ref, w_ref, out_ref, rest_ref):
    half = out_ref.shape[2]
    out_ref[:keep] = pack_ref[:keep]
    rest_ref[...] = pack_ref[keep:]
    for p in range(3):
        for q in range(3):
            for h in range(2):
                out_ref[keep + h * 9 + p * 3 + q] = w_ref[p, q, :, h * half : (h + 1) * half]


def early_kernel(early, near_ref, far_ref, wt_ref, xs_ref, part_ref):
    chans, lat = near_ref.shape[1:]
    wide = part_ref.shape[1] // 6
    batch, cols = wide // lat, xs_ref.shape[1] // wide
    pack = near_ref.shape[0] // 2
    weights_at = batch * cols + early

    for q in range(3):
        blocks = []
        for block in range(4):
            unit, ref = block % 2, near_ref if block < 2 else far_ref
            for p in range(3):
                first = unit * pack + weights_at + p * 3 + q
                blocks.append(jnp.concatenate([ref[first], ref[first + 9]], axis=1))
        for t in range(0, 12, 2):
            pair = jnp.concatenate(blocks[t : t + 2], axis=0)
            wt_ref[q, :, t * chans : (t + 2) * chans] = pair.T

    for block in range(4):
        unit, ref = block % 2, near_ref if block < 2 else far_ref
        for b in range(batch):
            for j in range(cols):
                x = ref[unit * pack + b * cols + j]
                place_block(xs_ref, block * 3 * chans, pl.ds(j * wide + b * lat, lat), x)

    for f in range(cols + 2):
        total = None
        for q in range(3):
            j = f + q - 2
            if 0 <= j < cols:
                term = jnp.dot(
                    wt_ref[q], xs_ref[:, j * wide : (j + 1) * wide], preferred_element_type=F32
                )
                total = term if total is None else total + term
        part_ref[:, f * wide : (f + 1) * wide] = total


def late_kernel(
    early, near_ref, far_ref, rim_ref, wt_ref, xs_ref, part_ref, wown_ref, cos_ref,
    gi_ref, wg_ref, loss_ref, xh_ref, tg_ref, cot_ref, grad_ref, sem,
):
    xhi, core = lax.axis_index("xhi"), lax.axis_index("core")
    batch, cols, chans, lat = gi_ref.shape
    wide = batch * lat
    tile = batch * cols
    rim = 3 * batch
    pack, rims = near_ref.shape[0] // 2, rim_ref.shape[0] // 2
    later = tile - early

    def outer(e):
        return e if e < 2 else e - cols

    for chip in range(2):
        for unit in range(2):
            row = (chip * 2 + unit) * 3 * chans
            trow = pl.multiple_of(((chip ^ xhi) * 2 + unit) * chans, chans)
            left = unit * rims + chip * rim
            main = near_ref if chip == 0 else far_ref
            right = left + 2 * rim
            for b in range(batch):
                for e in (0, 1, cols + 2, cols + 3):
                    x = rim_ref[left + b * 2 + e] if e < 2 else rim_ref[right + b * 2 + e - cols - 2]
                    place_block(xh_ref, row, pl.ds(outer(e) * wide + b * lat, lat), x)
                for f in range(cols + 2):
                    own = b * cols + f - 1
                    if f < 1:
                        t = rim_ref[left + 2 * batch + b]
                    elif f > cols:
                        t = rim_ref[right + 2 * batch + b]
                    elif own < early:
                        t = main[unit * pack + tile + own]
                    else:
                        t = rim_ref[unit * rims + 4 * rim + chip * later + own - early]
                    tg_ref[pl.ds(trow, chans), pl.ds(f * wide + b * lat, lat)] = t

    def column(e, rows):
        if 2 <= e < cols + 2:
            return xs_ref[rows, pl.ds((e - 2) * wide, wide)]
        return xh_ref[rows, pl.ds(outer(e) * wide, wide)]

    weighting = cos_ref[0:1, :]
    loss = jnp.zeros((8, wide), F32)
    for f in range(cols + 2):
        at = pl.ds(f * wide, wide)
        total = part_ref[:, at]
        for q in range(3):
            if not 2 <= f + q < cols + 2:
                total += jnp.dot(wt_ref[q], column(f + q, slice(None)), preferred_element_type=F32)
        diff = total - tg_ref[:, at].astype(F32)
        cot = weighting * diff
        cot_ref[:, at] = cot.astype(BF16)
        if 1 <= f <= cols:
            loss += jnp.sum((cot * diff).reshape(-1, 8, wide), axis=0)
    loss = jnp.sum(jnp.sum(loss, axis=1, keepdims=True), axis=0, keepdims=True)
    loss_ref[...] = jnp.broadcast_to(loss, loss_ref.shape)

    for j in range(cols):
        total = jnp.zeros((3 * chans, wide), F32)
        for q in range(3):
            total += jnp.dot(
                wown_ref[q], cot_ref[:, pl.ds((j + 2 - q) * wide, wide)], preferred_element_type=F32
            )
        for b in range(batch):
            part = total[:, b * lat : (b + 1) * lat]
            grad = (
                shift_lanes(part[:chans], 1)
                + part[chans : 2 * chans]
                + shift_lanes(part[2 * chans :], -1)
            )
            grad_ref[b, j] = grad.astype(BF16)
    leaving = pltpu.make_async_copy(grad_ref, gi_ref, sem)
    leaving.start()

    mine = pl.ds(pl.multiple_of(core * 3 * chans, chans), 3 * chans)
    half = wg_ref.shape[-1]
    total = None
    for j in range(cols):
        stack = jnp.concatenate([column(q + j + 1, mine) for q in range(3)], axis=0)
        term = lax.dot_general(
            stack,
            cot_ref[:, pl.ds((j + 1) * wide, wide)],
            (((1,), (1,)), ((), ())),
            preferred_element_type=F32,
        )
        total = term if total is None else total + term
    for q in range(3):
        for p in range(3):
            at = (q * 3 + p) * chans
            for h in range(2):
                wg_ref[h, p, q] = total[at : at + chans, h * half : (h + 1) * half].astype(BF16)
    leaving.wait()


def last_kernel(scale, halves_ref, value_ref, wg_ref, loss_ref):
    half = halves_ref.shape[-1]
    for h in range(2):
        wg_ref[:, :, :, h * half : (h + 1) * half] = halves_ref[h].astype(F32)
    loss_ref[0, 0] = jnp.max(value_ref[...]) * scale


def exchange(a, axes, count, to):
    return lax.ppermute(a, axes, [(i, to(i)) for i in range(count)])


def local(inputs, weights, target):
    batch, cols, chans, lat = inputs.shape
    channels = weights.shape[3]
    tiles = lax.axis_size(SPACE)
    lon = cols * tiles
    near, far = lax.axis_size(NEAR), lax.axis_size("zhi")

    def gathered(a):
        return lax.all_gather(a, "core", axis=0, tiled=True)

    own = jnp.concatenate(
        [inputs.reshape(-1, chans, lat), target.reshape(-1, chans, lat)], axis=0
    )
    other = exchange(own, "xhi", 2, lambda i: 1 - i)
    w_other = exchange(weights, ("xlo", "xhi"), 4, lambda i: 3 - i)

    def edge(pack, side):
        both = pack.reshape(2, batch, cols, chans, lat)
        if side > 0:
            x, t = both[0, :, cols - 2 :], both[1, :, cols - 1 :]
        else:
            x, t = both[0, :, :2], both[1, :, :1]
        return [x.reshape(-1, chans, lat), t.reshape(-1, chans, lat)]

    to_right = jnp.concatenate(edge(own, 1) + edge(other, 1), axis=0)
    to_left = jnp.concatenate(edge(own, -1) + edge(other, -1), axis=0)
    left = exchange(to_right, SPACE, tiles, lambda i: (i + 1) % tiles)
    right = exchange(to_left, SPACE, tiles, lambda i: (i - 1) % tiles)

    half = channels // 2
    tile, early = batch * cols, 5

    keep = tile + early
    vmem = pl.BlockSpec(memory_space=pltpu.VMEM)

    def with_weights(pack, w):
        return pl.pallas_call(
            functools.partial(pack_kernel, keep),
            out_shape=(
                jax.ShapeDtypeStruct((keep + 18, chans, half), BF16),
                jax.ShapeDtypeStruct((2 * tile - keep, chans, half), BF16),
            ),
            in_specs=[vmem] * 2,
            out_specs=(vmem, vmem),
            compiler_params=pltpu.CompilerParams(vmem_limit_bytes=8 * 1024 * 1024),
            cost_estimate=pl.CostEstimate(flops=0, bytes_accessed=1 << 20, transcendentals=0),
            name="pack",
        )(pack, w)

    near_part, near_rest = with_weights(own, weights)
    far_part, far_rest = with_weights(other, w_other)
    near_pack, far_pack = gathered(near_part), gathered(far_part)
    rim = gathered(jnp.concatenate([left, right, near_rest, far_rest], axis=0))
    wown = jnp.transpose(weights, (1, 0, 2, 3)).reshape(3, 3 * chans, channels)

    coslat = jnp.cos(jnp.pi * ((jnp.arange(lat, dtype=F32) + 0.5) / lat - 0.5))
    cos_rows = jnp.broadcast_to(jnp.tile(coslat, batch)[None], (8, batch * lat))

    wide = batch * lat
    wt, xs, part = pl.pallas_call(
        functools.partial(early_kernel, early),
        out_shape=(
            jax.ShapeDtypeStruct((3, channels, 3 * channels), BF16),
            jax.ShapeDtypeStruct((3 * channels, cols * wide), BF16),
            jax.ShapeDtypeStruct((channels, (cols + 2) * wide), F32),
        ),
        in_specs=[vmem] * 2,
        out_specs=(vmem, vmem, vmem),
        compiler_params=pltpu.CompilerParams(vmem_limit_bytes=16 * 1024 * 1024),
        cost_estimate=pl.CostEstimate(
            flops=24 * channels * channels * 3 * wide, bytes_accessed=6 << 20, transcendentals=0
        ),
        name="conv_tile",
    )(near_pack, far_pack)
    grad_input, wg, loss_part = pl.pallas_call(
        functools.partial(late_kernel, early),
        out_shape=(
            jax.ShapeDtypeStruct((batch, cols, chans, lat), BF16),
            jax.ShapeDtypeStruct((2, 3, 3, chans, half), BF16),
            jax.ShapeDtypeStruct((8, 128), F32),
        ),
        in_specs=[vmem] * 8,
        out_specs=(pl.BlockSpec(memory_space=pl.ANY), vmem, vmem),
        scratch_shapes=[
            pltpu.VMEM((3 * channels, 4 * wide), BF16),
            pltpu.VMEM((channels, (cols + 2) * wide), BF16),
            pltpu.VMEM((channels, (cols + 2) * wide), BF16),
            pltpu.VMEM((batch, cols, chans, lat), BF16),
            pltpu.SemaphoreType.DMA,
        ],
        compiler_params=pltpu.CompilerParams(vmem_limit_bytes=16 * 1024 * 1024),
        name="conv_rim",
    )(near_pack, far_pack, rim, wt, xs, part, wown, cos_rows)

    rows = 9 * chans * 2 // near
    parts = wg.reshape(near, rows, half)

    def with_loss(data, value):
        high = value.astype(BF16)
        low = (value - high.astype(F32)).astype(BF16)
        row = lax.broadcasted_iota(jnp.int32, value.shape, 0)
        block = jnp.where(row < 4, high, low)
        block = jnp.broadcast_to(block, data.shape[:1] + block.shape)
        return jnp.concatenate([data.astype(BF16), block], axis=1)

    def everyone(a, axes):
        return lax.all_to_all(a, axes, 0, 0, tiled=True)

    def summed(a):
        total = jnp.sum(a.astype(F32), axis=0)
        value = total[rows : rows + 4] + total[rows + 4 :]
        return total[:rows], value

    total, value = summed(everyone(with_loss(parts, loss_part), NEAR))
    spread = jnp.broadcast_to(total[None], (far, rows, half))
    total, value = summed(
        everyone(with_loss(spread, jnp.concatenate([value, value], axis=0)), "zhi")
    )
    total, value = lax.optimization_barrier((total, value))
    mine = (total * (scale_factor / (batch * lat * lon))).astype(BF16)
    third = everyone(jnp.broadcast_to(mine[None], (near, rows, half)), NEAR)
    weight_grad, loss = pl.pallas_call(
        functools.partial(last_kernel, 0.5 / (batch * lat * lon * channels)),
        out_shape=(
            jax.ShapeDtypeStruct(weights.shape, F32),
            jax.ShapeDtypeStruct((1, 1), F32),
        ),
        in_specs=[vmem] * 2,
        out_specs=(vmem, pl.BlockSpec(memory_space=pltpu.SMEM)),
        compiler_params=pltpu.CompilerParams(vmem_limit_bytes=8 * 1024 * 1024),
        name="widen",
    )(third.reshape(2, 3, 3, chans, half), value)
    return (loss[0, 0], grad_input, weight_grad)


def solution(mesh):
    grid = Mesh(mesh.devices.reshape(2, 4, 8, 2, 2, 2), SPACE + CHAN)
    in_specs = (
        P(None, SPACE, CHAN, None),
        P(None, None, CHAN, None),
        P(None, SPACE, CHAN, None),
    )
    out_specs = (P(), P(None, SPACE, CHAN, None), P(None, None, CHAN, None))
    return jax.shard_map(local, mesh=grid, in_specs=in_specs, out_specs=out_specs, check_vma=False)
```

```python
import functools

import jax
import jax.numpy as jnp
from jax import lax
from jax.experimental import pallas as pl
from jax.experimental.pallas import tpu as pltpu
from jax.sharding import Mesh
from jax.sharding import PartitionSpec as P

scale_factor = 64.0
SPACE = ("xlo", "y", "zhi", "zlo")
CHAN = ("xhi", "core")
NEAR = ("xlo", "y", "zlo")
BF16, F32 = jnp.bfloat16, jnp.float32


def shift_lanes(x, step):
    rows, lat = x.shape
    lane = lax.broadcasted_iota(jnp.int32, (rows, lat), 1)
    if step == 1:
        return jnp.where(lane == lat - 1, 0.0, pltpu.roll(x, lat - 1, 1))
    return jnp.where(lane == 0, 0.0, pltpu.roll(x, 1, 1))


def place_block(xs_ref, row, at, x):
    chans = x.shape[0]
    wide = x.astype(F32)
    xs_ref[row : row + chans, at] = shift_lanes(wide, -1).astype(BF16)
    xs_ref[row + chans : row + 2 * chans, at] = x
    xs_ref[row + 2 * chans : row + 3 * chans, at] = shift_lanes(wide, 1).astype(BF16)


def pack_kernel(keep, pack_ref, w_ref, out_ref, rest_ref):
    half = out_ref.shape[2]
    out_ref[:keep] = pack_ref[:keep]
    rest_ref[...] = pack_ref[keep:]
    for p in range(3):
        for q in range(3):
            for h in range(2):
                out_ref[keep + h * 9 + p * 3 + q] = w_ref[p, q, :, h * half : (h + 1) * half]


def early_kernel(early, near_ref, far_ref, wt_ref, xs_ref, part_ref):
    chans, lat = near_ref.shape[1:]
    wide = part_ref.shape[1] // 6
    batch, cols = wide // lat, xs_ref.shape[1] // wide
    pack = near_ref.shape[0] // 2
    weights_at = batch * cols + early

    for q in range(3):
        blocks = []
        for block in range(4):
            unit, ref = block % 2, near_ref if block < 2 else far_ref
            for p in range(3):
                first = unit * pack + weights_at + p * 3 + q
                blocks.append(jnp.concatenate([ref[first], ref[first + 9]], axis=1))
        for t in range(0, 12, 2):
            pair = jnp.concatenate(blocks[t : t + 2], axis=0)
            wt_ref[q, :, t * chans : (t + 2) * chans] = pair.T

    for block in range(4):
        unit, ref = block % 2, near_ref if block < 2 else far_ref
        for b in range(batch):
            for j in range(cols):
                x = ref[unit * pack + b * cols + j]
                place_block(xs_ref, block * 3 * chans, pl.ds(j * wide + b * lat, lat), x)

    for f in range(cols + 2):
        total = None
        for q in range(3):
            j = f + q - 2
            if 0 <= j < cols:
                term = jnp.dot(
                    wt_ref[q], xs_ref[:, j * wide : (j + 1) * wide], preferred_element_type=F32
                )
                total = term if total is None else total + term
        part_ref[:, f * wide : (f + 1) * wide] = total


def late_kernel(
    early, near_ref, far_ref, rim_ref, wt_ref, xs_ref, part_ref, wown_ref, cos_ref,
    gi_ref, wg_ref, loss_ref, xh_ref, tg_ref, cot_ref,
):
    xhi, core = lax.axis_index("xhi"), lax.axis_index("core")
    batch, cols, chans, lat = gi_ref.shape
    wide = batch * lat
    tile = batch * cols
    rim = 3 * batch
    pack, rims = near_ref.shape[0] // 2, rim_ref.shape[0] // 2
    later = tile - early

    def outer(e):
        return e if e < 2 else e - cols

    for chip in range(2):
        for unit in range(2):
            row = (chip * 2 + unit) * 3 * chans
            trow = pl.multiple_of(((chip ^ xhi) * 2 + unit) * chans, chans)
            left = unit * rims + chip * rim
            main = near_ref if chip == 0 else far_ref
            right = left + 2 * rim
            for b in range(batch):
                for e in (0, 1, cols + 2, cols + 3):
                    x = rim_ref[left + b * 2 + e] if e < 2 else rim_ref[right + b * 2 + e - cols - 2]
                    place_block(xh_ref, row, pl.ds(outer(e) * wide + b * lat, lat), x)
                for f in range(cols + 2):
                    own = b * cols + f - 1
                    if f < 1:
                        t = rim_ref[left + 2 * batch + b]
                    elif f > cols:
                        t = rim_ref[right + 2 * batch + b]
                    elif own < early:
                        t = main[unit * pack + tile + own]
                    else:
                        t = rim_ref[unit * rims + 4 * rim + chip * later + own - early]
                    tg_ref[pl.ds(trow, chans), pl.ds(f * wide + b * lat, lat)] = t

    def column(e, rows):
        if 2 <= e < cols + 2:
            return xs_ref[rows, pl.ds((e - 2) * wide, wide)]
        return xh_ref[rows, pl.ds(outer(e) * wide, wide)]

    weighting = cos_ref[0:1, :]
    loss = jnp.zeros((8, wide), F32)
    for f in range(cols + 2):
        at = pl.ds(f * wide, wide)
        total = part_ref[:, at]
        for q in range(3):
            if not 2 <= f + q < cols + 2:
                total += jnp.dot(wt_ref[q], column(f + q, slice(None)), preferred_element_type=F32)
        diff = total - tg_ref[:, at].astype(F32)
        cot = weighting * diff
        cot_ref[:, at] = cot.astype(BF16)
        if 1 <= f <= cols:
            loss += jnp.sum((cot * diff).reshape(-1, 8, wide), axis=0)
    loss = jnp.sum(jnp.sum(loss, axis=1, keepdims=True), axis=0, keepdims=True)
    loss_ref[...] = jnp.broadcast_to(loss, loss_ref.shape)

    for j in range(cols):
        total = jnp.zeros((3 * chans, wide), F32)
        for q in range(3):
            total += jnp.dot(
                wown_ref[q], cot_ref[:, pl.ds((j + 2 - q) * wide, wide)], preferred_element_type=F32
            )
        for b in range(batch):
            part = total[:, b * lat : (b + 1) * lat]
            grad = (
                shift_lanes(part[:chans], 1)
                + part[chans : 2 * chans]
                + shift_lanes(part[2 * chans :], -1)
            )
            gi_ref[b, j] = grad.astype(BF16)

    mine = pl.ds(pl.multiple_of(core * 3 * chans, chans), 3 * chans)
    half = wg_ref.shape[-1]
    total = None
    for j in range(cols):
        stack = jnp.concatenate([column(q + j + 1, mine) for q in range(3)], axis=0)
        term = lax.dot_general(
            stack,
            cot_ref[:, pl.ds((j + 1) * wide, wide)],
            (((1,), (1,)), ((), ())),
            preferred_element_type=F32,
        )
        total = term if total is None else total + term
    for q in range(3):
        for p in range(3):
            at = (q * 3 + p) * chans
            for h in range(2):
                wg_ref[h, p, q] = total[at : at + chans, h * half : (h + 1) * half].astype(BF16)


def last_kernel(scale, halves_ref, value_ref, wg_ref, loss_ref):
    half = halves_ref.shape[-1]
    for h in range(2):
        wg_ref[:, :, :, h * half : (h + 1) * half] = halves_ref[h].astype(F32)
    loss_ref[0, 0] = jnp.max(value_ref[...]) * scale


def exchange(a, axes, count, to):
    return lax.ppermute(a, axes, [(i, to(i)) for i in range(count)])


def local(inputs, weights, target):
    batch, cols, chans, lat = inputs.shape
    channels = weights.shape[3]
    tiles = lax.axis_size(SPACE)
    lon = cols * tiles
    near, far = lax.axis_size(NEAR), lax.axis_size("zhi")

    def gathered(a):
        return lax.all_gather(a, "core", axis=0, tiled=True)

    own = jnp.concatenate(
        [inputs.reshape(-1, chans, lat), target.reshape(-1, chans, lat)], axis=0
    )
    other = exchange(own, "xhi", 2, lambda i: 1 - i)
    w_other = exchange(weights, ("xlo", "xhi"), 4, lambda i: 3 - i)

    def edge(pack, side):
        both = pack.reshape(2, batch, cols, chans, lat)
        if side > 0:
            x, t = both[0, :, cols - 2 :], both[1, :, cols - 1 :]
        else:
            x, t = both[0, :, :2], both[1, :, :1]
        return [x.reshape(-1, chans, lat), t.reshape(-1, chans, lat)]

    to_right = jnp.concatenate(edge(own, 1) + edge(other, 1), axis=0)
    to_left = jnp.concatenate(edge(own, -1) + edge(other, -1), axis=0)
    left = exchange(to_right, SPACE, tiles, lambda i: (i + 1) % tiles)
    right = exchange(to_left, SPACE, tiles, lambda i: (i - 1) % tiles)

    half = channels // 2
    tile, early = batch * cols, 5

    keep = tile + early
    vmem = pl.BlockSpec(memory_space=pltpu.VMEM)

    def with_weights(pack, w):
        return pl.pallas_call(
            functools.partial(pack_kernel, keep),
            out_shape=(
                jax.ShapeDtypeStruct((keep + 18, chans, half), BF16),
                jax.ShapeDtypeStruct((2 * tile - keep, chans, half), BF16),
            ),
            in_specs=[vmem] * 2,
            out_specs=(vmem, vmem),
            compiler_params=pltpu.CompilerParams(vmem_limit_bytes=8 * 1024 * 1024),
            cost_estimate=pl.CostEstimate(flops=0, bytes_accessed=1 << 20, transcendentals=0),
            name="pack",
        )(pack, w)

    near_part, near_rest = with_weights(own, weights)
    far_part, far_rest = with_weights(other, w_other)
    near_pack, far_pack = gathered(near_part), gathered(far_part)
    rim = gathered(jnp.concatenate([left, right, near_rest, far_rest], axis=0))
    wown = jnp.transpose(weights, (1, 0, 2, 3)).reshape(3, 3 * chans, channels)

    coslat = jnp.cos(jnp.pi * ((jnp.arange(lat, dtype=F32) + 0.5) / lat - 0.5))
    cos_rows = jnp.broadcast_to(jnp.tile(coslat, batch)[None], (8, batch * lat))

    wide = batch * lat
    wt, xs, part = pl.pallas_call(
        functools.partial(early_kernel, early),
        out_shape=(
            jax.ShapeDtypeStruct((3, channels, 3 * channels), BF16),
            jax.ShapeDtypeStruct((3 * channels, cols * wide), BF16),
            jax.ShapeDtypeStruct((channels, (cols + 2) * wide), F32),
        ),
        in_specs=[vmem] * 2,
        out_specs=(vmem, vmem, vmem),
        compiler_params=pltpu.CompilerParams(vmem_limit_bytes=16 * 1024 * 1024),
        cost_estimate=pl.CostEstimate(
            flops=24 * channels * channels * 3 * wide, bytes_accessed=6 << 20, transcendentals=0
        ),
        name="conv_tile",
    )(near_pack, far_pack)
    grad_input, wg, loss_part = pl.pallas_call(
        functools.partial(late_kernel, early),
        out_shape=(
            jax.ShapeDtypeStruct((batch, cols, chans, lat), BF16),
            jax.ShapeDtypeStruct((2, 3, 3, chans, half), BF16),
            jax.ShapeDtypeStruct((8, 128), F32),
        ),
        in_specs=[vmem] * 8,
        out_specs=(vmem, vmem, vmem),
        scratch_shapes=[
            pltpu.VMEM((3 * channels, 4 * wide), BF16),
            pltpu.VMEM((channels, (cols + 2) * wide), BF16),
            pltpu.VMEM((channels, (cols + 2) * wide), BF16),
        ],
        compiler_params=pltpu.CompilerParams(vmem_limit_bytes=16 * 1024 * 1024),
        name="conv_rim",
    )(near_pack, far_pack, rim, wt, xs, part, wown, cos_rows)

    rows = 9 * chans * 2 // near
    parts = wg.reshape(near, rows, half)

    def with_loss(data, value):
        high = value.astype(BF16)
        low = (value - high.astype(F32)).astype(BF16)
        row = lax.broadcasted_iota(jnp.int32, value.shape, 0)
        block = jnp.where(row < 4, high, low)
        block = jnp.broadcast_to(block, data.shape[:1] + block.shape)
        return jnp.concatenate([data.astype(BF16), block], axis=1)

    def everyone(a, axes):
        return lax.all_to_all(a, axes, 0, 0, tiled=True)

    def summed(a):
        total = jnp.sum(a.astype(F32), axis=0)
        value = total[rows : rows + 4] + total[rows + 4 :]
        return total[:rows], value

    total, value = summed(everyone(with_loss(parts, loss_part), NEAR))
    spread = jnp.broadcast_to(total[None], (far, rows, half))
    total, value = summed(
        everyone(with_loss(spread, jnp.concatenate([value, value], axis=0)), "zhi")
    )
    total, value = lax.optimization_barrier((total, value))
    mine = (total * (scale_factor / (batch * lat * lon))).astype(BF16)
    third = everyone(jnp.broadcast_to(mine[None], (near, rows, half)), NEAR)
    weight_grad, loss = pl.pallas_call(
        functools.partial(last_kernel, 0.5 / (batch * lat * lon * channels)),
        out_shape=(
            jax.ShapeDtypeStruct(weights.shape, F32),
            jax.ShapeDtypeStruct((1, 1), F32),
        ),
        in_specs=[vmem] * 2,
        out_specs=(vmem, pl.BlockSpec(memory_space=pltpu.SMEM)),
        compiler_params=pltpu.CompilerParams(vmem_limit_bytes=8 * 1024 * 1024),
        name="widen",
    )(third.reshape(2, 3, 3, chans, half), value)
    return (loss[0, 0], grad_input, weight_grad)


def solution(mesh):
    grid = Mesh(mesh.devices.reshape(2, 4, 8, 2, 2, 2), SPACE + CHAN)
    in_specs = (
        P(None, SPACE, CHAN, None),
        P(None, None, CHAN, None),
        P(None, SPACE, CHAN, None),
    )
    out_specs = (P(), P(None, SPACE, CHAN, None), P(None, None, CHAN, None))
    return jax.shard_map(local, mesh=grid, in_specs=in_specs, out_specs=out_specs, check_vma=False)
```

```python
import functools

import jax
import jax.numpy as jnp
from jax import lax
from jax.experimental import pallas as pl
from jax.experimental.pallas import tpu as pltpu
from jax.sharding import Mesh
from jax.sharding import PartitionSpec as P

scale_factor = 64.0
SPACE = ("xlo", "y", "zhi", "zlo")
CHAN = ("xhi", "core")
NEAR = ("xlo", "y", "zlo")
BF16, F32 = jnp.bfloat16, jnp.float32


def shift_lanes(x, step):
    rows, lat = x.shape
    lane = lax.broadcasted_iota(jnp.int32, (rows, lat), 1)
    if step == 1:
        return jnp.where(lane == lat - 1, 0.0, pltpu.roll(x, lat - 1, 1))
    return jnp.where(lane == 0, 0.0, pltpu.roll(x, 1, 1))


def place_block(xs_ref, row, at, x):
    chans = x.shape[0]
    wide = x.astype(F32)
    xs_ref[row : row + chans, at] = shift_lanes(wide, -1).astype(BF16)
    xs_ref[row + chans : row + 2 * chans, at] = x
    xs_ref[row + 2 * chans : row + 3 * chans, at] = shift_lanes(wide, 1).astype(BF16)


def pack_kernel(keep, pack_ref, w_ref, out_ref, rest_ref):
    half = out_ref.shape[2]
    out_ref[:keep] = pack_ref[:keep]
    rest_ref[...] = pack_ref[keep:]
    for p in range(3):
        for q in range(3):
            for h in range(2):
                out_ref[keep + h * 9 + p * 3 + q] = w_ref[p, q, :, h * half : (h + 1) * half]


def early_kernel(early, near_ref, far_ref, wt_ref, xs_ref, part_ref):
    chans, lat = near_ref.shape[1:]
    wide = part_ref.shape[1] // 6
    batch, cols = wide // lat, xs_ref.shape[1] // wide
    pack = near_ref.shape[0] // 2
    weights_at = batch * cols + early

    for q in range(3):
        blocks = []
        for block in range(4):
            unit, ref = block % 2, near_ref if block < 2 else far_ref
            for p in range(3):
                first = unit * pack + weights_at + p * 3 + q
                blocks.append(jnp.concatenate([ref[first], ref[first + 9]], axis=1))
        for t in range(0, 12, 2):
            pair = jnp.concatenate(blocks[t : t + 2], axis=0)
            wt_ref[q, :, t * chans : (t + 2) * chans] = pair.T

    for block in range(4):
        unit, ref = block % 2, near_ref if block < 2 else far_ref
        for b in range(batch):
            for j in range(cols):
                x = ref[unit * pack + b * cols + j]
                place_block(xs_ref, block * 3 * chans, pl.ds(j * wide + b * lat, lat), x)

    for f in range(cols + 2):
        total = None
        for q in range(3):
            j = f + q - 2
            if 0 <= j < cols:
                term = jnp.dot(
                    wt_ref[q], xs_ref[:, j * wide : (j + 1) * wide], preferred_element_type=F32
                )
                total = term if total is None else total + term
        part_ref[:, f * wide : (f + 1) * wide] = total


def late_kernel(
    early, near_ref, far_ref, rim_ref, wt_ref, xs_ref, part_ref, wown_ref, cos_ref,
    gi_ref, wg_ref, loss_ref, xh_ref, tg_ref, cot_ref,
):
    xhi, core = lax.axis_index("xhi"), lax.axis_index("core")
    batch, cols, chans, lat = gi_ref.shape
    wide = batch * lat
    tile = batch * cols
    rim = 3 * batch
    pack, rims = near_ref.shape[0] // 2, rim_ref.shape[0] // 2
    later = tile - early

    def outer(e):
        return e if e < 2 else e - cols

    for chip in range(2):
        for unit in range(2):
            row = (chip * 2 + unit) * 3 * chans
            trow = pl.multiple_of(((chip ^ xhi) * 2 + unit) * chans, chans)
            left = unit * rims + chip * rim
            main = near_ref if chip == 0 else far_ref
            right = left + 2 * rim
            for b in range(batch):
                for e in (0, 1, cols + 2, cols + 3):
                    x = rim_ref[left + b * 2 + e] if e < 2 else rim_ref[right + b * 2 + e - cols - 2]
                    place_block(xh_ref, row, pl.ds(outer(e) * wide + b * lat, lat), x)
                for f in range(cols + 2):
                    own = b * cols + f - 1
                    if f < 1:
                        t = rim_ref[left + 2 * batch + b]
                    elif f > cols:
                        t = rim_ref[right + 2 * batch + b]
                    elif own < early:
                        t = main[unit * pack + tile + own]
                    else:
                        t = rim_ref[unit * rims + 4 * rim + chip * later + own - early]
                    tg_ref[pl.ds(trow, chans), pl.ds(f * wide + b * lat, lat)] = t

    def column(e, rows):
        if 2 <= e < cols + 2:
            return xs_ref[rows, pl.ds((e - 2) * wide, wide)]
        return xh_ref[rows, pl.ds(outer(e) * wide, wide)]

    weighting = cos_ref[0:1, :]
    loss = jnp.zeros((8, wide), F32)
    for f in range(cols + 2):
        at = pl.ds(f * wide, wide)
        total = part_ref[:, at]
        for q in range(3):
            if not 2 <= f + q < cols + 2:
                total += jnp.dot(wt_ref[q], column(f + q, slice(None)), preferred_element_type=F32)
        diff = total - tg_ref[:, at].astype(F32)
        cot = weighting * diff
        cot_ref[:, at] = cot.astype(BF16)
        if 1 <= f <= cols:
            loss += jnp.sum((cot * diff).reshape(-1, 8, wide), axis=0)
    loss = jnp.sum(jnp.sum(loss, axis=1, keepdims=True), axis=0, keepdims=True)
    loss_ref[...] = jnp.broadcast_to(loss, loss_ref.shape)

    for j in range(cols):
        total = jnp.zeros((3 * chans, wide), F32)
        for q in range(3):
            total += jnp.dot(
                wown_ref[q], cot_ref[:, pl.ds((j + 2 - q) * wide, wide)], preferred_element_type=F32
            )
        for b in range(batch):
            part = total[:, b * lat : (b + 1) * lat]
            grad = (
                shift_lanes(part[:chans], 1)
                + part[chans : 2 * chans]
                + shift_lanes(part[2 * chans :], -1)
            )
            gi_ref[b, j] = grad.astype(BF16)

    mine = pl.ds(pl.multiple_of(core * 3 * chans, chans), 3 * chans)
    half = wg_ref.shape[-1]
    total = None
    for j in range(cols):
        stack = jnp.concatenate([column(q + j + 1, mine) for q in range(3)], axis=0)
        term = lax.dot_general(
            stack,
            cot_ref[:, pl.ds((j + 1) * wide, wide)],
            (((1,), (1,)), ((), ())),
            preferred_element_type=F32,
        )
        total = term if total is None else total + term
    for q in range(3):
        for p in range(3):
            at = (q * 3 + p) * chans
            for h in range(2):
                wg_ref[h, p, q] = total[at : at + chans, h * half : (h + 1) * half].astype(BF16)


def last_kernel(scale, halves_ref, value_ref, wg_ref, loss_ref):
    half = halves_ref.shape[-1]
    for h in range(2):
        wg_ref[:, :, :, h * half : (h + 1) * half] = halves_ref[h].astype(F32)
    loss_ref[0, 0] = jnp.max(value_ref[...]) * scale


def exchange(a, axes, count, to):
    return lax.ppermute(a, axes, [(i, to(i)) for i in range(count)])


def local(inputs, weights, target):
    batch, cols, chans, lat = inputs.shape
    channels = weights.shape[3]
    tiles = lax.axis_size(SPACE)
    lon = cols * tiles
    near, far = lax.axis_size(NEAR), lax.axis_size("zhi")

    def gathered(a):
        return lax.all_gather(a, "core", axis=0, tiled=True)

    own = jnp.concatenate(
        [inputs.reshape(-1, chans, lat), target.reshape(-1, chans, lat)], axis=0
    )
    other = exchange(own, "xhi", 2, lambda i: 1 - i)
    w_other = exchange(weights, ("xlo", "xhi"), 4, lambda i: 3 - i)

    def edge(pack, side):
        both = pack.reshape(2, batch, cols, chans, lat)
        if side > 0:
            x, t = both[0, :, cols - 2 :], both[1, :, cols - 1 :]
        else:
            x, t = both[0, :, :2], both[1, :, :1]
        return [x.reshape(-1, chans, lat), t.reshape(-1, chans, lat)]

    to_right = jnp.concatenate(edge(own, 1) + edge(other, 1), axis=0)
    to_left = jnp.concatenate(edge(own, -1) + edge(other, -1), axis=0)
    left = exchange(to_right, SPACE, tiles, lambda i: (i + 1) % tiles)
    right = exchange(to_left, SPACE, tiles, lambda i: (i - 1) % tiles)

    half = channels // 2
    tile, early = batch * cols, 6

    keep = tile + early
    vmem = pl.BlockSpec(memory_space=pltpu.VMEM)

    def with_weights(pack, w):
        return pl.pallas_call(
            functools.partial(pack_kernel, keep),
            out_shape=(
                jax.ShapeDtypeStruct((keep + 18, chans, half), BF16),
                jax.ShapeDtypeStruct((2 * tile - keep, chans, half), BF16),
            ),
            in_specs=[vmem] * 2,
            out_specs=(vmem, vmem),
            compiler_params=pltpu.CompilerParams(vmem_limit_bytes=8 * 1024 * 1024),
            cost_estimate=pl.CostEstimate(flops=0, bytes_accessed=1 << 20, transcendentals=0),
            name="pack",
        )(pack, w)

    near_part, near_rest = with_weights(own, weights)
    far_part, far_rest = with_weights(other, w_other)
    near_pack, far_pack = gathered(near_part), gathered(far_part)
    rim = gathered(jnp.concatenate([left, right, near_rest, far_rest], axis=0))
    wown = jnp.transpose(weights, (1, 0, 2, 3)).reshape(3, 3 * chans, channels)

    coslat = jnp.cos(jnp.pi * ((jnp.arange(lat, dtype=F32) + 0.5) / lat - 0.5))
    cos_rows = jnp.broadcast_to(jnp.tile(coslat, batch)[None], (8, batch * lat))

    wide = batch * lat
    wt, xs, part = pl.pallas_call(
        functools.partial(early_kernel, early),
        out_shape=(
            jax.ShapeDtypeStruct((3, channels, 3 * channels), BF16),
            jax.ShapeDtypeStruct((3 * channels, cols * wide), BF16),
            jax.ShapeDtypeStruct((channels, (cols + 2) * wide), F32),
        ),
        in_specs=[vmem] * 2,
        out_specs=(vmem, vmem, vmem),
        compiler_params=pltpu.CompilerParams(vmem_limit_bytes=16 * 1024 * 1024),
        cost_estimate=pl.CostEstimate(
            flops=24 * channels * channels * 3 * wide, bytes_accessed=6 << 20, transcendentals=0
        ),
        name="conv_tile",
    )(near_pack, far_pack)
    grad_input, wg, loss_part = pl.pallas_call(
        functools.partial(late_kernel, early),
        out_shape=(
            jax.ShapeDtypeStruct((batch, cols, chans, lat), BF16),
            jax.ShapeDtypeStruct((2, 3, 3, chans, half), BF16),
            jax.ShapeDtypeStruct((8, 128), F32),
        ),
        in_specs=[vmem] * 8,
        out_specs=(vmem, vmem, vmem),
        scratch_shapes=[
            pltpu.VMEM((3 * channels, 4 * wide), BF16),
            pltpu.VMEM((channels, (cols + 2) * wide), BF16),
            pltpu.VMEM((channels, (cols + 2) * wide), BF16),
        ],
        compiler_params=pltpu.CompilerParams(vmem_limit_bytes=16 * 1024 * 1024),
        name="conv_rim",
    )(near_pack, far_pack, rim, wt, xs, part, wown, cos_rows)

    rows = 9 * chans * 2 // near
    parts = wg.reshape(near, rows, half)

    def with_loss(data, value):
        high = value.astype(BF16)
        low = (value - high.astype(F32)).astype(BF16)
        row = lax.broadcasted_iota(jnp.int32, value.shape, 0)
        block = jnp.where(row < 4, high, low)
        block = jnp.broadcast_to(block, data.shape[:1] + block.shape)
        return jnp.concatenate([data.astype(BF16), block], axis=1)

    def everyone(a, axes):
        return lax.all_to_all(a, axes, 0, 0, tiled=True)

    def summed(a):
        total = jnp.sum(a.astype(F32), axis=0)
        value = total[rows : rows + 4] + total[rows + 4 :]
        return total[:rows], value

    total, value = summed(everyone(with_loss(parts, loss_part), NEAR))
    spread = jnp.broadcast_to(total[None], (far, rows, half))
    total, value = summed(
        everyone(with_loss(spread, jnp.concatenate([value, value], axis=0)), "zhi")
    )
    total, value = lax.optimization_barrier((total, value))
    mine = (total * (scale_factor / (batch * lat * lon))).astype(BF16)
    third = everyone(jnp.broadcast_to(mine[None], (near, rows, half)), NEAR)
    weight_grad, loss = pl.pallas_call(
        functools.partial(last_kernel, 0.5 / (batch * lat * lon * channels)),
        out_shape=(
            jax.ShapeDtypeStruct(weights.shape, F32),
            jax.ShapeDtypeStruct((1, 1), F32),
        ),
        in_specs=[vmem] * 2,
        out_specs=(vmem, pl.BlockSpec(memory_space=pltpu.SMEM)),
        compiler_params=pltpu.CompilerParams(vmem_limit_bytes=8 * 1024 * 1024),
        name="widen",
    )(third.reshape(2, 3, 3, chans, half), value)
    return (loss[0, 0], grad_input, weight_grad)


def solution(mesh):
    grid = Mesh(mesh.devices.reshape(2, 4, 8, 2, 2, 2), SPACE + CHAN)
    in_specs = (
        P(None, SPACE, CHAN, None),
        P(None, None, CHAN, None),
        P(None, SPACE, CHAN, None),
    )
    out_specs = (P(), P(None, SPACE, CHAN, None), P(None, None, CHAN, None))
    return jax.shard_map(local, mesh=grid, in_specs=in_specs, out_specs=out_specs, check_vma=False)
```
